512 devices in a mesh: prefix: 32 (over x, y, core), sample: 16 (over z).
Axes of the slice: x: 4, y: 4, z: 16, core: 2. Of those that a mesh axis runs over, the one named last changes fastest.
Arguments:
- queries: bfloat16 [64, 8192], P('sample'), may hold values from -100 to 100
- pool_keys: bfloat16 [2048, 128, 1024], P(('prefix', 'sample')), may hold values from -6 to 6
- pool_values: bfloat16 [2048, 128, 1024], P(('prefix', 'sample')), may hold values from -6 to 6
- page_prompt: int32 [2048], P(('prefix', 'sample')), may hold values from -1 to 3, as said below
- suffix_keys: bfloat16 [64, 1024, 1024], P('sample', 'prefix'), may hold values from -6 to 6
- suffix_values: bfloat16 [64, 1024, 1024], P('sample', 'prefix'), may hold values from -6 to 6
- suffix_len: int32 [64], P('sample'), may hold values from 1 to 1024, as said below
Outputs:
- attention_out: bfloat16 [64, 8192], P('sample', 'prefix')
The draws below stay inside these ranges and needn't reach their ends.
Inputs may be any that keep to these rules, and one draw needn't show every extreme that they name: `page_prompt`: each of the 4 prompts is held by exactly 256 slots; every other slot holds -1. `suffix_len`: the longest suffix is exactly 1024.
All inputs are finite; a program needn't handle non-finite values.
Results may differ from the reference program's by a relative error of at most 0.0065.
Values may be sent and summed in bfloat16 or wider, within the bound.
No kernel may reach another device: no remote copies, remote signals or barrier semaphores. Data moves between devices by JAX's collectives and lax.ppermute only.
A program may use at most 64 MiB of HBM per device.

```python
import math
import jax
import jax.numpy as jnp
from jax import lax

H = 64
KVH = 8
HD = 128
PAGE = 128
G = 4
SPP = 16
SUF = 1024
SLOTS = 2048
PAGES_PROMPT = 256
B = 64


def owner_table(key):
    owner_key = jax.random.fold_in(key, 101)
    permuted = jax.random.permutation(owner_key, SLOTS)
    ranks = jnp.arange(SLOTS, dtype=jnp.int32)
    used_slots = G * PAGES_PROMPT
    prompt_of_rank = jnp.where(ranks < used_slots, ranks // PAGES_PROMPT, -1).astype(jnp.int32)
    return prompt_of_rank[permuted]


def draw_page_prompt(key, part):
    return owner_table(key)


def draw_pool_keys(key, part):
    key = jax.random.fold_in(key, 5)
    noise_field = jax.random.normal(key, (SLOTS, PAGE, KVH, HD), jnp.float32)
    return jnp.clip(noise_field, -6.0, 6.0).reshape(SLOTS, PAGE, KVH * HD).astype(jnp.bfloat16)


def draw_queries(key, part):
    key = jax.random.fold_in(key, 7)
    query_noise = jax.random.normal(key, (B, H, HD), jnp.float32)
    result = jnp.clip(2.5 * query_noise, -15.0, 15.0)
    return result.reshape(B, H * HD).astype(jnp.bfloat16)


def draw_suffix_len(key, part):
    key = jax.random.fold_in(key, 9)
    length_draw = jax.random.randint(key, (B,), 1, SUF + 1)
    longest = jax.random.randint(jax.random.fold_in(key, 1), (), 0, B)
    return length_draw.at[longest].set(SUF).astype(jnp.int32)


def block_levels(own_key, shape, split, least, high):
    level, own = 1.0, jax.random.fold_in(own_key, 6)
    for position, shards_of in split:
        heights = jnp.exp(jax.random.uniform(jax.random.fold_in(own, position), (shards_of,), jnp.float32, least / len(split), high / len(split)))
        level = level * jnp.repeat(heights, shape[position] // shards_of).reshape([-1 if axis == position else 1 for axis in range(len(shape))])
    return level


def bell_draw(rng, dims, deviation, limit, shards=(), kind=jnp.bfloat16):
    drawn = deviation * jax.random.normal(rng, dims, jnp.float32)
    if shards:
        drawn = drawn * block_levels(rng, dims, shards, -0.22, 0.18)
    return jnp.clip(drawn, -limit, limit).astype(kind)


def setup_inputs(seed: int = 0) -> dict:
    arg_keys = jax.random.split(jax.random.key(seed), 8)
    return {
        "queries": draw_queries(jax.random.fold_in(arg_keys[7], 71), 0),
        "pool_keys": draw_pool_keys(jax.random.fold_in(arg_keys[7], 71), 0),
        "pool_values": bell_draw(arg_keys[2], (SLOTS, PAGE, KVH * HD), 1.0, 6.0, ((0, 512),)),
        "page_prompt": draw_page_prompt(jax.random.fold_in(arg_keys[7], 71), 0),
        "suffix_keys": bell_draw(arg_keys[4], (B, SUF, KVH * HD), 1.0, 6.0, ((0, 16), (1, 32))),
        "suffix_values": bell_draw(arg_keys[5], (B, SUF, KVH * HD), 1.0, 6.0, ((0, 16), (1, 32))),
        "suffix_len": draw_suffix_len(jax.random.fold_in(arg_keys[7], 71), 0),
    }


NEG_FILL = -1e+30

def rounded(weights):
    narrow = weights.astype(jnp.bfloat16)
    narrow = lax.optimization_barrier(narrow)
    return narrow.astype(jnp.float32)

def reference(queries, pool_keys, pool_values, page_prompt, suffix_keys, suffix_values, suffix_len):
    group_size = H // KVH
    score_scale = 1.0 / math.sqrt(HD)
    query_grid = queries.astype(jnp.float32).reshape(G, SPP, KVH, group_size, HD)
    positions = jnp.arange(SUF, dtype=jnp.int32)
    highest = lax.Precision.HIGHEST

    def one_prompt(prompt_index):
        slot_ids = jnp.nonzero(page_prompt == prompt_index, size=PAGES_PROMPT)[0].astype(jnp.int32)
        key_rows = pool_keys[slot_ids].astype(jnp.float32).reshape(PAGES_PROMPT * PAGE, KVH, HD)
        value_rows = pool_values[slot_ids].astype(jnp.float32).reshape(PAGES_PROMPT * PAGE, KVH, HD)
        query_block = lax.dynamic_index_in_dim(query_grid, prompt_index, 0, keepdims=False)
        row_start = (prompt_index * SPP).astype(jnp.int32)
        suffix_key_rows = lax.dynamic_slice_in_dim(suffix_keys, row_start, SPP, 0).astype(jnp.float32).reshape(SPP, SUF, KVH, HD)
        suffix_value_rows = lax.dynamic_slice_in_dim(suffix_values, row_start, SPP, 0).astype(jnp.float32).reshape(SPP, SUF, KVH, HD)
        lengths = lax.dynamic_slice_in_dim(suffix_len, row_start, SPP, 0)
        live_mask = (positions[None, :] < lengths[:, None])[:, None, None, :]
        prefix_scores = jnp.einsum('sagd,tad->sagt', query_block, key_rows, precision=highest) * score_scale
        suffix_scores = jnp.einsum('sagd,stad->sagt', query_block, suffix_key_rows, precision=highest) * score_scale
        suffix_scores = jnp.where(live_mask, suffix_scores, NEG_FILL)
        row_peak = jnp.maximum(prefix_scores.max(-1), suffix_scores.max(-1))
        prefix_weights = jnp.exp(prefix_scores - row_peak[..., None])
        suffix_weights = jnp.where(live_mask, jnp.exp(suffix_scores - row_peak[..., None]), 0.0)
        denominator = prefix_weights.sum(-1) + suffix_weights.sum(-1)
        numerator = jnp.einsum('sagt,tad->sagd', rounded(prefix_weights), value_rows, precision=highest)
        numerator = numerator + jnp.einsum('sagt,stad->sagd', rounded(suffix_weights), suffix_value_rows, precision=highest)
        mixed = numerator / denominator[..., None]
        return mixed.astype(jnp.bfloat16).reshape(SPP, H * HD)
    outputs = lax.map(one_prompt, jnp.arange(G, dtype=jnp.int32))
    return outputs.reshape(G * SPP, H * HD)
```

```python
import math

import jax
import jax.numpy as jnp
from jax import lax
from jax.experimental import pallas as pl
from jax.experimental.pallas import tpu as pltpu
from jax.sharding import PartitionSpec as P

H = 64
KVH = 8
HD = 128
PAGE = 128
SPP = 16
PROMPTS = 4
CORES = 2
OWN = 4
SPAN = 32
PLANE = 16
DEPTH = 16
ROWS = 128
HEAD_ROWS = 64
STAT_ROWS = 32
BLOCK_ROWS = ROWS + STAT_ROWS
SEND_ROWS = 2 * PAGE + 2 * SPAN + 16
NEG = -1e30
MIB = 1 << 20
SCALE = math.log2(math.e) / math.sqrt(HD)
F32 = jnp.float32
BF16 = jnp.bfloat16


def stage_kernel(page_prompt, queries, pool_keys, pool_values, suffix_keys, suffix_values,
                 query_out, send_out, sems):
    core = lax.rem(lax.axis_index("prefix"), CORES)
    pieces = ((pool_keys, 0, PAGE), (pool_values, PAGE, PAGE),
              (suffix_keys, 2 * PAGE, SPAN), (suffix_values, 2 * PAGE + SPAN, SPAN))
    copies = [
        pltpu.make_async_copy(src, send_out.at[:, pl.ds(start, rows), :], sems.at[i])
        for i, (src, start, rows) in enumerate(pieces)
    ]
    for copy in copies:
        copy.start()
    for slot in range(OWN):
        mark = jnp.full((16, KVH * HD), page_prompt[slot], jnp.int32)
        send_out[slot, pl.ds(2 * PAGE + 2 * SPAN, 16), :] = mark.astype(F32).astype(BF16)
    for a in range(KVH):
        parts = []
        for half in range(2):
            for mate in range(2):
                head = a * 8 + half * 4 + mate
                column = pl.multiple_of(head * HD + core * (2 * HD), HD)
                parts.append(queries[:, pl.ds(column, HD)].astype(F32))
        rows = jnp.concatenate(parts, axis=0).astype(BF16)
        for plane in range(DEPTH):
            query_out[plane, pl.ds(a * 16, 16), :] = rows
    for copy in copies:
        copy.wait()


def attend_kernel(page_prompt, suffix_len, queries_hbm, keys_hbm, values_hbm, suffix_keys_hbm,
                  suffix_values_hbm, got_hbm, out, queries, keys, values, suffix_keys,
                  suffix_values, marks, prompts, scores, top, peak, total, acc, sems):
    prefix = lax.axis_index("prefix")
    plane = lax.axis_index("sample")
    pairs = (
        (got_hbm.at[:, pl.ds(2 * PAGE + 2 * SPAN, 16), pl.ds(0, HD)], marks),
        (queries_hbm, queries),
        (keys_hbm, keys.at[pl.ds(0, OWN)]),
        (got_hbm.at[:, pl.ds(0, PAGE), :], keys.at[pl.ds(OWN, OWN)]),
        (suffix_keys_hbm, suffix_keys.at[0]),
        (got_hbm.at[:, pl.ds(2 * PAGE, SPAN), :], suffix_keys.at[1]),
        (values_hbm, values.at[pl.ds(0, OWN)]),
        (got_hbm.at[:, pl.ds(PAGE, PAGE), :], values.at[pl.ds(OWN, OWN)]),
        (suffix_values_hbm, suffix_values.at[0]),
        (got_hbm.at[:, pl.ds(2 * PAGE + SPAN, SPAN), :], suffix_values.at[1]),
    )
    copies = [pltpu.make_async_copy(src, dst, sems.at[i]) for i, (src, dst) in enumerate(pairs)]
    for copy in copies:
        copy.start()
    top[...] = jnp.full(top.shape, NEG, F32)
    total[...] = jnp.zeros(total.shape, F32)
    acc[...] = jnp.zeros(acc.shape, F32)

    copies[0].wait()
    for slot in range(OWN):
        prompts[slot] = page_prompt[slot]
        prompts[OWN + slot] = jnp.max(marks[slot].astype(F32)).astype(jnp.int32)

    own_prompt = lax.div(plane, 4)
    quarter = lax.rem(plane, 4)
    row = lax.broadcasted_iota(jnp.int32, (HEAD_ROWS, PAGE), 0)
    token = lax.broadcasted_iota(jnp.int32, (HEAD_ROWS, PAGE), 1)
    token_sample = token >> 5
    length = jnp.where(
        token_sample == 0, suffix_len[0],
        jnp.where(token_sample == 1, suffix_len[1],
                  jnp.where(token_sample == 2, suffix_len[2], suffix_len[3])))
    mine = ((row >> 4) == quarter) & ((row & 3) == token_sample)

    def live(part):
        owner = prefix if part == 0 else prefix + 1 - 2 * lax.rem(prefix, CORES)
        return mine & (owner * SPAN + (token & (SPAN - 1)) < length)

    def query_rows(prompt, a):
        rows = queries[pl.ds(prompt * 4, 4), pl.ds(a * 16, 16), :]
        return rows.reshape(HEAD_ROWS, HD)

    def dot_keys(prompt, a, key):
        return SCALE * lax.dot_general(
            query_rows(prompt, a), key, (((1,), (1,)), ((), ())), preferred_element_type=F32)

    for copy in copies[1:6]:
        copy.wait()

    @pl.loop(0, 2 * OWN)
    def _(slot):
        prompt = prompts[slot]

        @pl.when(prompt >= 0)
        def _():
            for a in range(KVH):
                s = dot_keys(prompt, a, keys[slot, :, pl.ds(a * HD, HD)])
                scores[slot, a] = s
                top[prompt, a] = jnp.maximum(top[prompt, a], s)

    for part in range(2):
        mask = live(part)
        for a in range(KVH):
            key = suffix_keys[part, :, :, pl.ds(a * HD, HD)].reshape(OWN * SPAN, HD)
            s = jnp.where(mask, dot_keys(own_prompt, a, key), NEG)
            scores[2 * OWN + part, a] = s
            top[own_prompt, a] = jnp.maximum(top[own_prompt, a], s)

    @pl.loop(0, PROMPTS)
    def _(prompt):
        for a in range(KVH):
            best = jnp.max(top[prompt, a], axis=1, keepdims=True)
            best = best.astype(BF16).astype(F32)
            peak[prompt, a] = jnp.broadcast_to(best, (HEAD_ROWS, HD))

    for copy in copies[6:]:
        copy.wait()

    @pl.loop(0, 2 * OWN)
    def _(slot):
        prompt = prompts[slot]

        @pl.when(prompt >= 0)
        def _():
            for a in range(KVH):
                w = jnp.exp2(scores[slot, a] - peak[prompt, a])
                total[prompt, a] += w
                acc[prompt, a] += jnp.dot(
                    w.astype(BF16), values[slot, :, pl.ds(a * HD, HD)],
                    preferred_element_type=F32)

    for part in range(2):
        mask = live(part)
        for a in range(KVH):
            value = suffix_values[part, :, :, pl.ds(a * HD, HD)].reshape(OWN * SPAN, HD)
            w = jnp.where(mask, jnp.exp2(scores[2 * OWN + part, a] - peak[own_prompt, a]), 0.0)
            total[own_prompt, a] += w
            acc[own_prompt, a] += jnp.dot(w.astype(BF16), value, preferred_element_type=F32)

    lane = lax.broadcasted_iota(jnp.int32, (HEAD_ROWS, HD), 1)

    @pl.loop(0, KVH)
    def _(a):
        stats = jnp.zeros((HEAD_ROWS, HD), F32)
        for prompt in range(PROMPTS):
            low = jnp.sum(total[prompt, a], axis=1, keepdims=True)
            high = low.astype(BF16).astype(F32)
            stats = jnp.where(lane == prompt, peak[prompt, a], stats)
            stats = jnp.where(lane == 4 + prompt, high, stats)
            stats = jnp.where(lane == 8 + prompt, low - high, stats)
        for half in range(2):
            def pick(tile):
                return jnp.concatenate(
                    [tile[q * 16 + half * 8:q * 16 + half * 8 + 8] for q in range(4)], axis=0)
            for prompt in range(PROMPTS):
                out[a * 2 + half, pl.ds(prompt * 32, 32), :] = pick(acc[prompt, a]).astype(BF16)
            out[a * 2 + half, pl.ds(ROWS, STAT_ROWS), :] = pick(stats).astype(BF16)


def plane_kernel(got, out):
    best = jnp.full((STAT_ROWS, HD), NEG, F32)
    for src in range(PLANE):
        best = jnp.maximum(best, got[src, pl.ds(ROWS, STAT_ROWS), :].astype(F32))
    denominator = jnp.zeros((STAT_ROWS, HD), F32)
    sums = [jnp.zeros((STAT_ROWS, HD), F32) for _ in range(PROMPTS)]
    for src in range(PLANE):
        stats = got[src, pl.ds(ROWS, STAT_ROWS), :].astype(F32)
        weight = jnp.exp2(jnp.minimum(stats - best, 0.0))
        part = pltpu.roll(stats, HD - 4, 1) + pltpu.roll(stats, HD - 8, 1)
        denominator = denominator + weight * part
        for prompt in range(PROMPTS):
            tile = got[src, pl.ds(prompt * 32, 32), :].astype(F32)
            sums[prompt] = sums[prompt] + tile * weight[:, prompt:prompt + 1]
    lane = lax.broadcasted_iota(jnp.int32, (8, HD), 1)
    for prompt in range(PROMPTS):
        for quarter in range(4):
            rows = slice(quarter * 8, quarter * 8 + 8)
            stat = jnp.where(lane == 0, best[rows, prompt:prompt + 1],
                             denominator[rows, prompt:prompt + 1])
            out[prompt * 4 + quarter, pl.ds(0, 8), :] = sums[prompt][rows]
            out[prompt * 4 + quarter, pl.ds(8, 8), :] = stat


def final_kernel(got, out):
    best = got[0, pl.ds(8, 8), :]
    for src in range(1, DEPTH):
        best = jnp.maximum(best, got[src, pl.ds(8, 8), :])
    best = best[:, 0:1]
    denominator = jnp.zeros((8, 1), F32)
    numerator = jnp.zeros((8, HD), F32)
    for src in range(DEPTH):
        stat = got[src, pl.ds(8, 8), :]
        weight = jnp.exp2(stat[:, 0:1] - best)
        denominator = denominator + weight * stat[:, 1:2]
        numerator = numerator + weight * got[src, pl.ds(0, 8), :]
    mixed = (numerator / denominator).astype(BF16)
    out[...] = jnp.concatenate([mixed[0:4], mixed[4:8]], axis=1)


SMEM = pl.BlockSpec(memory_space=pltpu.SMEM)
VMEM = pl.BlockSpec(memory_space=pltpu.VMEM)
ANY = pl.BlockSpec(memory_space=pl.ANY)


def body(queries, pool_keys, pool_values, page_prompt, suffix_keys, suffix_values, suffix_len):
    width = KVH * HD
    query_blocks, send = pl.pallas_call(
        stage_kernel,
        out_shape=(jax.ShapeDtypeStruct((DEPTH, ROWS, HD), BF16),
                   jax.ShapeDtypeStruct((OWN, SEND_ROWS, width), BF16)),
        in_specs=[SMEM, VMEM, ANY, ANY, ANY, ANY],
        out_specs=(VMEM, VMEM),
        scratch_shapes=[pltpu.SemaphoreType.DMA((4,))],
        compiler_params=pltpu.CompilerParams(vmem_limit_bytes=6 * MIB),
        name="stage",
    )(page_prompt, queries, pool_keys, pool_values, suffix_keys, suffix_values)
    got = lax.ppermute(send, "prefix", [(i, i ^ 1) for i in range(CORES * PLANE)])
    every_query = lax.all_to_all(query_blocks, "sample", 0, 0)
    partial = pl.pallas_call(
        attend_kernel,
        out_shape=jax.ShapeDtypeStruct((PLANE, BLOCK_ROWS, HD), BF16),
        in_specs=[SMEM, SMEM] + [ANY] * 6,
        out_specs=VMEM,
        scratch_shapes=[
            pltpu.VMEM((DEPTH, ROWS, HD), BF16),
            pltpu.VMEM((2 * OWN, PAGE, width), BF16),
            pltpu.VMEM((2 * OWN, PAGE, width), BF16),
            pltpu.VMEM((2, OWN, SPAN, width), BF16),
            pltpu.VMEM((2, OWN, SPAN, width), BF16),
            pltpu.VMEM((OWN, 16, HD), BF16),
            pltpu.SMEM((2 * OWN,), jnp.int32),
            pltpu.VMEM((2 * OWN + 2, KVH, HEAD_ROWS, PAGE), F32),
            pltpu.VMEM((PROMPTS, KVH, HEAD_ROWS, PAGE), F32),
            pltpu.VMEM((PROMPTS, KVH, HEAD_ROWS, HD), F32),
            pltpu.VMEM((PROMPTS, KVH, HEAD_ROWS, PAGE), F32),
            pltpu.VMEM((PROMPTS, KVH, HEAD_ROWS, HD), F32),
            pltpu.SemaphoreType.DMA((10,)),
        ],
        compiler_params=pltpu.CompilerParams(vmem_limit_bytes=16 * MIB),
        name="attend",
    )(page_prompt, suffix_len, every_query, pool_keys, pool_values, suffix_keys, suffix_values, got)
    same_core = [[chip * CORES + core for chip in range(PLANE)] for core in range(CORES)]
    partial = lax.all_to_all(partial, "prefix", 0, 0, axis_index_groups=same_core)
    summed = pl.pallas_call(
        plane_kernel,
        out_shape=jax.ShapeDtypeStruct((DEPTH, 16, HD), F32),
        in_specs=[VMEM],
        out_specs=VMEM,
        compiler_params=pltpu.CompilerParams(vmem_limit_bytes=4 * MIB),
        name="plane",
    )(partial)
    summed = lax.all_to_all(summed, "sample", 0, 0)
    return pl.pallas_call(
        final_kernel,
        out_shape=jax.ShapeDtypeStruct((OWN, 2 * HD), BF16),
        in_specs=[VMEM],
        out_specs=VMEM,
        compiler_params=pltpu.CompilerParams(vmem_limit_bytes=2 * MIB),
        name="final",
    )(summed)


def solution(mesh):
    placed = (
        P("sample", None),
        P(("prefix", "sample"), None, None),
        P(("prefix", "sample"), None, None),
        P(("prefix", "sample")),
        P("sample", "prefix", None),
        P("sample", "prefix", None),
        P("sample"),
    )
    return jax.shard_map(
        body, mesh=mesh, in_specs=placed, out_specs=P("sample", "prefix"), check_vma=False
    )
```

```python
import math

import jax
import jax.numpy as jnp
from jax import lax
from jax.experimental import pallas as pl
from jax.experimental.pallas import tpu as pltpu
from jax.sharding import PartitionSpec as P

H = 64
KVH = 8
HD = 128
PAGE = 128
SPP = 16
PROMPTS = 4
CORES = 2
OWN = 4
SPAN = 32
PLANE = 16
DEPTH = 16
ROWS = 128
HEAD_ROWS = 64
STAT_ROWS = 32
BLOCK_ROWS = ROWS + STAT_ROWS
KEY_ROW = 0
VALUE_ROW = PAGE
SUFFIX_KEY_ROW = 2 * PAGE
SUFFIX_VALUE_ROW = 2 * PAGE + SPAN
MARK_ROW = 2 * PAGE + 2 * SPAN
SEND_ROWS = MARK_ROW + 16
NEG = -1e30
MIB = 1 << 20
SCALE = math.log2(math.e) / math.sqrt(HD)
F32 = jnp.float32
BF16 = jnp.bfloat16


def query_kernel(queries, out):
    core = lax.rem(lax.axis_index("prefix"), CORES)
    for a in range(KVH):
        parts = []
        for half in range(2):
            for mate in range(2):
                head = a * 8 + half * 4 + mate
                column = pl.multiple_of(head * HD + core * (2 * HD), HD)
                parts.append(queries[:, pl.ds(column, HD)].astype(F32))
        out[pl.ds(a * 16, 16), :] = jnp.concatenate(parts, axis=0).astype(BF16)


def copy_kernel(shifted, out):
    rows = shifted[...]
    for chip in range(PLANE):
        out[chip] = rows


def stage_kernel(page_prompt, pool_keys, pool_values, suffix_keys, suffix_values, out,
                 prompts, sems):
    pieces = ((pool_keys, KEY_ROW, PAGE), (pool_values, VALUE_ROW, PAGE),
              (suffix_keys, SUFFIX_KEY_ROW, SPAN), (suffix_values, SUFFIX_VALUE_ROW, SPAN))
    copies = [
        pltpu.make_async_copy(src, out.at[:, pl.ds(start, rows), :], sems.at[i])
        for i, (src, start, rows) in enumerate(pieces)
    ]
    prompt_copy = pltpu.make_async_copy(page_prompt, prompts, sems.at[4])
    prompt_copy.start()
    for copy in copies:
        copy.start()
    prompt_copy.wait()
    for slot in range(OWN):
        mark = jnp.full((16, KVH * HD), prompts[slot], jnp.int32)
        out[slot, pl.ds(MARK_ROW, 16), :] = mark.astype(F32).astype(BF16)
    for copy in copies:
        copy.wait()


def attend_kernel(page_prompt, suffix_len, queries, held, got, out,
                  scores, top, peak, total, acc):
    prefix = lax.axis_index("prefix")
    plane = lax.axis_index("sample")
    top[...] = jnp.full(top.shape, NEG, F32)
    total[...] = jnp.zeros(total.shape, F32)
    acc[...] = jnp.zeros(acc.shape, F32)

    prompts = [page_prompt[slot] for slot in range(OWN)]
    for slot in range(OWN):
        mark = got[slot, pl.ds(MARK_ROW, 16), pl.ds(0, HD)].astype(F32)
        prompts.append(jnp.max(mark).astype(jnp.int32))
    held_prompts = [jnp.maximum(prompt, 0) for prompt in prompts]

    own_prompt = lax.div(plane, 4)
    quarter = lax.rem(plane, 4)
    row = lax.broadcasted_iota(jnp.int32, (HEAD_ROWS, PAGE), 0)
    token = lax.broadcasted_iota(jnp.int32, (HEAD_ROWS, PAGE), 1)
    token_sample = token >> 5
    length = jnp.where(
        token_sample == 0, suffix_len[0],
        jnp.where(token_sample == 1, suffix_len[1],
                  jnp.where(token_sample == 2, suffix_len[2], suffix_len[3])))
    mine = ((row >> 4) == quarter) & ((row & 3) == token_sample)

    def live(part):
        owner = prefix if part == 0 else prefix + 1 - 2 * lax.rem(prefix, CORES)
        return mine & (owner * SPAN + (token & (SPAN - 1)) < length)

    def query_rows(prompt, a):
        return jnp.concatenate(
            [queries[(plane - prompt * 4 - q) & (DEPTH - 1), pl.ds(a * 16, 16), :]
             for q in range(4)], axis=0)

    def dot_keys(prompt, a, key):
        return SCALE * lax.dot_general(
            query_rows(prompt, a), key, (((1,), (1,)), ((), ())), preferred_element_type=F32)

    for part, pages in enumerate((held, got)):
        for slot in range(part * OWN, (part + 1) * OWN):
            for a in range(KVH):
                key = pages[slot % OWN, pl.ds(KEY_ROW, PAGE), pl.ds(a * HD, HD)]
                s = dot_keys(held_prompts[slot], a, key)
                s = jnp.where(prompts[slot] >= 0, s, NEG)
                scores[slot, a] = s
                top[held_prompts[slot], a] = jnp.maximum(top[held_prompts[slot], a], s)

    for part, pages in enumerate((held, got)):
        mask = live(part)
        for a in range(KVH):
            key = pages[:, pl.ds(SUFFIX_KEY_ROW, SPAN), pl.ds(a * HD, HD)]
            key = key.reshape(OWN * SPAN, HD)
            s = jnp.where(mask, dot_keys(own_prompt, a, key), NEG)
            scores[2 * OWN + part, a] = s
            top[own_prompt, a] = jnp.maximum(top[own_prompt, a], s)

    @pl.loop(0, PROMPTS)
    def _(prompt):
        for a in range(KVH):
            best = jnp.max(top[prompt, a], axis=1, keepdims=True)
            best = best.astype(BF16).astype(F32)
            peak[prompt, a] = jnp.broadcast_to(best, (HEAD_ROWS, HD))

    for part, pages in enumerate((held, got)):
        for slot in range(part * OWN, (part + 1) * OWN):
            prompt = held_prompts[slot]
            for a in range(KVH):
                value = pages[slot % OWN, pl.ds(VALUE_ROW, PAGE), pl.ds(a * HD, HD)]
                w = jnp.exp2(scores[slot, a] - peak[prompt, a])
                w = jnp.where(prompts[slot] >= 0, w, 0.0)
                total[prompt, a] += w
                acc[prompt, a] += jnp.dot(w.astype(BF16), value, preferred_element_type=F32)

    for part, pages in enumerate((held, got)):
        mask = live(part)
        for a in range(KVH):
            value = pages[:, pl.ds(SUFFIX_VALUE_ROW, SPAN), pl.ds(a * HD, HD)]
            value = value.reshape(OWN * SPAN, HD)
            w = jnp.where(mask, jnp.exp2(scores[2 * OWN + part, a] - peak[own_prompt, a]), 0.0)
            total[own_prompt, a] += w
            acc[own_prompt, a] += jnp.dot(w.astype(BF16), value, preferred_element_type=F32)

    lane = lax.broadcasted_iota(jnp.int32, (HEAD_ROWS, HD), 1)

    @pl.loop(0, KVH)
    def _(a):
        stats = jnp.zeros((HEAD_ROWS, HD), F32)
        for prompt in range(PROMPTS):
            low = jnp.sum(total[prompt, a], axis=1, keepdims=True)
            high = low.astype(BF16).astype(F32)
            stats = jnp.where(lane == prompt, peak[prompt, a], stats)
            stats = jnp.where(lane == 4 + prompt, high, stats)
            stats = jnp.where(lane == 8 + prompt, low - high, stats)
        for half in range(2):
            def pick(tile):
                return jnp.concatenate(
                    [tile[q * 16 + half * 8:q * 16 + half * 8 + 8] for q in range(4)], axis=0)
            for prompt in range(PROMPTS):
                out[a * 2 + half, pl.ds(prompt * 32, 32), :] = pick(acc[prompt, a]).astype(BF16)
            out[a * 2 + half, pl.ds(ROWS, STAT_ROWS), :] = pick(stats).astype(BF16)


def plane_kernel(got, out):
    best = jnp.full((STAT_ROWS, HD), NEG, F32)
    for src in range(PLANE):
        best = jnp.maximum(best, got[src, pl.ds(ROWS, STAT_ROWS), :].astype(F32))
    denominator = jnp.zeros((STAT_ROWS, HD), F32)
    sums = [jnp.zeros((STAT_ROWS, HD), F32) for _ in range(PROMPTS)]
    for src in range(PLANE):
        stats = got[src, pl.ds(ROWS, STAT_ROWS), :].astype(F32)
        weight = jnp.exp2(jnp.minimum(stats - best, 0.0))
        part = pltpu.roll(stats, HD - 4, 1) + pltpu.roll(stats, HD - 8, 1)
        denominator = denominator + weight * part
        for prompt in range(PROMPTS):
            tile = got[src, pl.ds(prompt * 32, 32), :].astype(F32)
            sums[prompt] = sums[prompt] + tile * weight[:, prompt:prompt + 1]
    lane = lax.broadcasted_iota(jnp.int32, (8, HD), 1)
    for prompt in range(PROMPTS):
        for quarter in range(4):
            rows = slice(quarter * 8, quarter * 8 + 8)
            stat = jnp.where(lane == 0, best[rows, prompt:prompt + 1],
                             denominator[rows, prompt:prompt + 1])
            out[prompt * 4 + quarter, pl.ds(0, 8), :] = sums[prompt][rows]
            out[prompt * 4 + quarter, pl.ds(8, 8), :] = stat


def final_kernel(got, out):
    best = got[0, pl.ds(8, 8), :]
    for src in range(1, DEPTH):
        best = jnp.maximum(best, got[src, pl.ds(8, 8), :])
    best = best[:, 0:1]
    denominator = jnp.zeros((8, 1), F32)
    numerator = jnp.zeros((8, HD), F32)
    for src in range(DEPTH):
        stat = got[src, pl.ds(8, 8), :]
        weight = jnp.exp2(stat[:, 0:1] - best)
        denominator = denominator + weight * stat[:, 1:2]
        numerator = numerator + weight * got[src, pl.ds(0, 8), :]
    mixed = (numerator / denominator).astype(BF16)
    out[...] = jnp.concatenate([mixed[0:4], mixed[4:8]], axis=1)


SMEM = pl.BlockSpec(memory_space=pltpu.SMEM)
VMEM = pl.BlockSpec(memory_space=pltpu.VMEM)
ANY = pl.BlockSpec(memory_space=pl.ANY)


def budget(mib):
    return pltpu.CompilerParams(vmem_limit_bytes=int(mib * MIB))


def body(queries, pool_keys, pool_values, page_prompt, suffix_keys, suffix_values, suffix_len):
    own_queries = pl.pallas_call(
        query_kernel,
        out_shape=jax.ShapeDtypeStruct((ROWS, HD), BF16),
        in_specs=[VMEM],
        out_specs=VMEM,
        compiler_params=budget(2),
        name="query",
    )(queries)
    held = pl.pallas_call(
        stage_kernel,
        out_shape=jax.ShapeDtypeStruct((OWN, SEND_ROWS, KVH * HD), BF16),
        in_specs=[ANY] * 5,
        out_specs=VMEM,
        scratch_shapes=[pltpu.SMEM((OWN,), jnp.int32), pltpu.SemaphoreType.DMA((5,))],
        compiler_params=budget(4),
        name="stage",
    )(*(pltpu.with_memory_space_constraint(array, pltpu.HBM)
        for array in (page_prompt, pool_keys, pool_values, suffix_keys, suffix_values)))
    shifted = lax.ppermute(
        own_queries, ("prefix", "sample"),
        [((chip * CORES + core) * DEPTH + z, (chip * CORES + core) * DEPTH + (z + chip) % DEPTH)
         for chip in range(PLANE) for core in range(CORES) for z in range(DEPTH)])
    got = lax.ppermute(held, "prefix", [(i, i ^ 1) for i in range(CORES * PLANE)])
    same_core = [[chip * CORES + core for chip in range(PLANE)] for core in range(CORES)]
    copies = pl.pallas_call(
        copy_kernel,
        out_shape=jax.ShapeDtypeStruct((PLANE, ROWS, HD), BF16),
        in_specs=[VMEM],
        out_specs=VMEM,
        compiler_params=budget(2),
        cost_estimate=pl.CostEstimate(flops=10**11, transcendentals=0, bytes_accessed=MIB),
        name="copies",
    )(shifted)
    every_query = lax.all_to_all(copies, "prefix", 0, 0, axis_index_groups=same_core)
    partial = pl.pallas_call(
        attend_kernel,
        out_shape=jax.ShapeDtypeStruct((PLANE, BLOCK_ROWS, HD), BF16),
        in_specs=[SMEM, SMEM, VMEM, VMEM, VMEM],
        out_specs=VMEM,
        scratch_shapes=[
            pltpu.VMEM((2 * OWN + 2, KVH, HEAD_ROWS, PAGE), F32),
            pltpu.VMEM((PROMPTS, KVH, HEAD_ROWS, PAGE), F32),
            pltpu.VMEM((PROMPTS, KVH, HEAD_ROWS, HD), F32),
            pltpu.VMEM((PROMPTS, KVH, HEAD_ROWS, PAGE), F32),
            pltpu.VMEM((PROMPTS, KVH, HEAD_ROWS, HD), F32),
        ],
        compiler_params=budget(18),
        name="attend",
    )(page_prompt, suffix_len, every_query, held, got)
    partial = lax.all_to_all(partial, "prefix", 0, 0, axis_index_groups=same_core)
    summed = pl.pallas_call(
        plane_kernel,
        out_shape=jax.ShapeDtypeStruct((DEPTH, 16, HD), F32),
        in_specs=[VMEM],
        out_specs=VMEM,
        compiler_params=budget(4),
        name="plane",
    )(partial)
    summed = lax.all_to_all(summed, "sample", 0, 0)
    return pl.pallas_call(
        final_kernel,
        out_shape=jax.ShapeDtypeStruct((OWN, 2 * HD), BF16),
        in_specs=[VMEM],
        out_specs=VMEM,
        compiler_params=budget(2),
        name="final",
    )(summed)


def solution(mesh):
    placed = (
        P("sample", None),
        P(("prefix", "sample"), None, None),
        P(("prefix", "sample"), None, None),
        P(("prefix", "sample")),
        P("sample", "prefix", None),
        P("sample", "prefix", None),
        P("sample"),
    )
    return jax.shard_map(
        body, mesh=mesh, in_specs=placed, out_specs=P("sample", "prefix"), check_vma=False
    )
```

```python
import math

import jax
import jax.numpy as jnp
from jax import lax
from jax.experimental import pallas as pl
from jax.experimental.pallas import tpu as pltpu
from jax.sharding import PartitionSpec as P

H = 64
KVH = 8
HD = 128
PAGE = 128
SPP = 16
PROMPTS = 4
CORES = 2
OWN = 4
SPAN = 32
PLANE = 16
DEPTH = 16
ROWS = 128
HEAD_ROWS = 64
STAT_ROWS = 16
BLOCK_ROWS = ROWS + STAT_ROWS
KEY_ROW = 0
VALUE_ROW = PAGE
SUFFIX_KEY_ROW = 2 * PAGE
SUFFIX_VALUE_ROW = 2 * PAGE + SPAN
MARK_ROW = 2 * PAGE + 2 * SPAN
SEND_ROWS = MARK_ROW + 16
NEG = -1e30
MIB = 1 << 20
SCALE = math.log2(math.e) / math.sqrt(HD)
CHIP_ORDER = (0, 4, 1, 2, 8, 3, 12, 5, 6, 9, 13, 7, 14, 11, 10, 15)
DISTANCES = (8, 7, 9, 6, 10, 5, 11, 4, 12, 3, 13, 2, 14, 1, 15, 0)
DISTANCE_OF = dict(zip(CHIP_ORDER, DISTANCES))
CHIP_OF = dict(zip(DISTANCES, CHIP_ORDER))
F32 = jnp.float32
BF16 = jnp.bfloat16


def query_kernel(queries, out):
    core = lax.rem(lax.axis_index("prefix"), CORES)
    for a in range(KVH):
        parts = []
        for half in range(2):
            for mate in range(2):
                head = a * 8 + half * 4 + mate
                column = pl.multiple_of(head * HD + core * (2 * HD), HD)
                parts.append(queries[:, pl.ds(column, HD)].astype(F32))
        out[pl.ds(a * 16, 16), :] = jnp.concatenate(parts, axis=0).astype(BF16)


def copy_kernel(shifted, out):
    rows = shifted[...]
    for chip in range(PLANE):
        out[chip] = rows


def stage_kernel(page_prompt, pool_keys, pool_values, suffix_keys, suffix_values, out,
                 keys, suffix, prompts, sems):
    pieces = ((page_prompt, prompts), (pool_keys, keys), (suffix_keys, suffix),
              (pool_values, out.at[:, pl.ds(VALUE_ROW, PAGE), :]),
              (suffix_values, out.at[:, pl.ds(SUFFIX_VALUE_ROW, SPAN), :]))
    copies = [pltpu.make_async_copy(src, dst, sems.at[i]) for i, (src, dst) in enumerate(pieces)]
    for copy in copies:
        copy.start()
    copies[0].wait()
    for slot in range(OWN):
        mark = jnp.full((16, KVH * HD), prompts[slot], jnp.int32)
        out[slot, pl.ds(MARK_ROW, 16), :] = mark.astype(F32).astype(BF16)
    copies[1].wait()
    for slot in range(OWN):
        for a in range(KVH):
            head = pl.ds(a * HD, HD)
            out[slot, pl.ds(KEY_ROW, PAGE), head] = keys[slot, :, head].T
    copies[2].wait()
    for a in range(KVH):
        head = pl.ds(a * HD, HD)
        turned = suffix[:, :, head].reshape(OWN * SPAN, HD).T
        out[:, pl.ds(SUFFIX_KEY_ROW, SPAN), head] = turned.reshape(OWN, SPAN, OWN * SPAN)
    for copy in copies[3:]:
        copy.wait()


def attend_kernel(page_prompt, suffix_len, chip_of, queries, held, got, out, scores,
                  suffix_scores, *buffers):
    top, peak, total, acc = (buffers[i * KVH:(i + 1) * KVH] for i in range(4))
    prefix = lax.axis_index("prefix")
    plane = lax.axis_index("sample")
    sign = 1 - 2 * lax.rem(prefix, CORES)
    for a in range(KVH):
        top[a][...] = jnp.full(top[a].shape, NEG, F32)
        total[a][...] = jnp.zeros(total[a].shape, F32)
        acc[a][...] = jnp.zeros(acc[a].shape, F32)
        peak[a][PROMPTS] = jnp.zeros((HEAD_ROWS, HD), F32)

    prompts = [page_prompt[slot] for slot in range(OWN)]
    for slot in range(OWN):
        mark = got[slot, pl.ds(MARK_ROW, 16), pl.ds(0, HD)].astype(F32)
        prompts.append(jnp.max(mark).astype(jnp.int32))
    prompts = [jnp.where(prompt >= 0, prompt, PROMPTS) for prompt in prompts]

    own_prompt = lax.div(plane, 4)
    quarter = lax.rem(plane, 4)
    row = lax.broadcasted_iota(jnp.int32, (16, PAGE), 0)
    token = lax.broadcasted_iota(jnp.int32, (16, PAGE), 1)
    token_sample = token >> 5
    length = jnp.where(
        token_sample == 0, suffix_len[0],
        jnp.where(token_sample == 1, suffix_len[1],
                  jnp.where(token_sample == 2, suffix_len[2], suffix_len[3])))
    own_rows = pl.ds(pl.multiple_of(quarter * 16, 16), 16)

    def live(part):
        owner = prefix if part == 0 else prefix + sign
        position = owner * SPAN + (token & (SPAN - 1))
        return ((row & 3) == token_sample) & (position < length)

    def chip_rows(sample_plane, a):
        chip = chip_of[(sign * (plane - sample_plane)) & (DEPTH - 1)]
        return queries[chip, pl.ds(a * 16, 16), :]

    def query_rows(prompt, a):
        return jnp.concatenate([chip_rows(prompt * 4 + q, a) for q in range(4)], axis=0)

    def dot_keys(rows, key):
        return SCALE * lax.dot_general(
            rows, key, (((1,), (0,)), ((), ())), preferred_element_type=F32)

    for part, pages in enumerate((held, got)):
        for slot in range(part * OWN, (part + 1) * OWN):
            for a in range(KVH):
                key = pages[slot % OWN, pl.ds(KEY_ROW, PAGE), pl.ds(a * HD, HD)]
                s = dot_keys(query_rows(prompts[slot], a), key)
                scores[slot, a] = s
                top[a][prompts[slot]] = jnp.maximum(top[a][prompts[slot]], s)

    for part, pages in enumerate((held, got)):
        mask = live(part)
        for a in range(KVH):
            key = pages[:, pl.ds(SUFFIX_KEY_ROW, SPAN), pl.ds(a * HD, HD)]
            key = key.reshape(HD, OWN * SPAN)
            s = jnp.where(mask, dot_keys(chip_rows(plane, a), key), NEG)
            suffix_scores[part, a] = s
            top[a][own_prompt, own_rows] = jnp.maximum(top[a][own_prompt, own_rows], s)

    for a in range(KVH):
        for prompt in range(PROMPTS):
            best = jnp.max(top[a][prompt], axis=1, keepdims=True)
            best = best.astype(BF16).astype(F32)
            peak[a][prompt] = jnp.broadcast_to(best, (HEAD_ROWS, HD))

    for part, pages in enumerate((held, got)):
        for slot in range(part * OWN, (part + 1) * OWN):
            prompt = prompts[slot]
            for a in range(KVH):
                value = pages[slot % OWN, pl.ds(VALUE_ROW, PAGE), pl.ds(a * HD, HD)]
                w = jnp.exp2(scores[slot, a] - peak[a][prompt])
                total[a][prompt] += w
                acc[a][prompt] += jnp.dot(w.astype(BF16), value, preferred_element_type=F32)

    for part, pages in enumerate((held, got)):
        mask = live(part)
        for a in range(KVH):
            value = pages[:, pl.ds(SUFFIX_VALUE_ROW, SPAN), pl.ds(a * HD, HD)]
            value = value.reshape(OWN * SPAN, HD)
            w = jnp.exp2(suffix_scores[part, a] - peak[a][own_prompt, own_rows])
            w = jnp.where(mask, w, 0.0)
            total[a][own_prompt, own_rows] += w
            acc[a][own_prompt, own_rows] += jnp.dot(
                w.astype(BF16), value, preferred_element_type=F32)

    lane = lax.broadcasted_iota(jnp.int32, (HEAD_ROWS, HD), 1)

    for a in range(KVH):
        stats = jnp.zeros((HEAD_ROWS, HD), F32)
        for prompt in range(PROMPTS):
            low = jnp.sum(total[a][prompt], axis=1, keepdims=True)
            high = low.astype(BF16).astype(F32)
            stats = jnp.where(lane == prompt, peak[a][prompt], stats)
            stats = jnp.where(lane == 4 + prompt, high, stats)
            stats = jnp.where(lane == 8 + prompt, low - high, stats)
        for half in range(2):
            def quarter_rows(tile, q):
                return tile[q * 16 + half * 8:q * 16 + half * 8 + 8]
            for prompt in range(PROMPTS):
                sums = acc[a][prompt]
                rows = jnp.concatenate([quarter_rows(sums, q) for q in range(4)], axis=0)
                out[a * 2 + half, pl.ds(prompt * 32, 32), :] = rows.astype(BF16)
            packed = jnp.concatenate(
                [quarter_rows(stats, q) + pltpu.roll(quarter_rows(stats, q + 1), 16, 1)
                 for q in (0, 2)], axis=0)
            out[a * 2 + half, pl.ds(ROWS, STAT_ROWS), :] = packed.astype(BF16)


def plane_kernel(got, out):
    stats = [got[src, pl.ds(ROWS, STAT_ROWS), :].astype(F32) for src in range(PLANE)]
    best = stats[0]
    for src in range(1, PLANE):
        best = jnp.maximum(best, stats[src])
    denominator = jnp.zeros((STAT_ROWS, HD), F32)
    sums = [jnp.zeros((8, HD), F32) for _ in range(DEPTH)]

    def column(tile, prompt, quarter):
        rows, start = quarter // 2 * 8, quarter % 2 * 16 + prompt
        return tile[rows:rows + 8, start:start + 1]

    for src in range(PLANE):
        weight = jnp.exp2(jnp.minimum(stats[src] - best, 0.0))
        part = pltpu.roll(stats[src], HD - 4, 1) + pltpu.roll(stats[src], HD - 8, 1)
        denominator = denominator + weight * part
        for prompt in range(PROMPTS):
            tile = got[src, pl.ds(prompt * 32, 32), :].astype(F32)
            for quarter in range(4):
                i = prompt * 4 + quarter
                sums[i] = sums[i] + (
                    tile[quarter * 8:quarter * 8 + 8] * column(weight, prompt, quarter))
    high = denominator.astype(BF16).astype(F32)
    lane = lax.broadcasted_iota(jnp.int32, (8, HD), 1)
    for prompt in range(PROMPTS):
        for quarter in range(4):
            i = prompt * 4 + quarter
            stat = jnp.where(
                lane == 0, column(best, prompt, quarter),
                jnp.where(lane == 1, column(high, prompt, quarter),
                          column(denominator - high, prompt, quarter)))
            out[i] = jnp.concatenate([sums[i], stat], axis=0).astype(BF16)


def final_kernel(got, out):
    tiles = [got[src].astype(F32) for src in range(DEPTH)]
    best = tiles[0][8:16]
    for src in range(1, DEPTH):
        best = jnp.maximum(best, tiles[src][8:16])
    best = best[:, 0:1]
    denominator = jnp.zeros((8, 1), F32)
    numerator = jnp.zeros((8, HD), F32)
    for tile in tiles:
        stat = tile[8:16]
        weight = jnp.exp2(stat[:, 0:1] - best)
        denominator = denominator + weight * (stat[:, 1:2] + stat[:, 2:3])
        numerator = numerator + weight * tile[0:8]
    mixed = (numerator / denominator).astype(BF16)
    out[...] = jnp.concatenate([mixed[0:4], mixed[4:8]], axis=1)


SMEM = pl.BlockSpec(memory_space=pltpu.SMEM)
VMEM = pl.BlockSpec(memory_space=pltpu.VMEM)
ANY = pl.BlockSpec(memory_space=pl.ANY)


def budget(mib):
    return pltpu.CompilerParams(vmem_limit_bytes=int(mib * MIB))


def body(queries, pool_keys, pool_values, page_prompt, suffix_keys, suffix_values, suffix_len):
    own_queries = pl.pallas_call(
        query_kernel,
        out_shape=jax.ShapeDtypeStruct((ROWS, HD), BF16),
        in_specs=[VMEM],
        out_specs=VMEM,
        compiler_params=budget(2),
        name="query",
    )(queries)
    held = pl.pallas_call(
        stage_kernel,
        out_shape=jax.ShapeDtypeStruct((OWN, SEND_ROWS, KVH * HD), BF16),
        in_specs=[ANY] * 5,
        out_specs=VMEM,
        scratch_shapes=[
            pltpu.VMEM((OWN, PAGE, KVH * HD), BF16),
            pltpu.VMEM((OWN, SPAN, KVH * HD), BF16),
            pltpu.SMEM((OWN,), jnp.int32),
            pltpu.SemaphoreType.DMA((5,)),
        ],
        compiler_params=budget(6),
        name="stage",
    )(*(pltpu.with_memory_space_constraint(array, pltpu.HBM)
        for array in (page_prompt, pool_keys, pool_values, suffix_keys, suffix_values)))
    shifted = lax.ppermute(
        own_queries, ("prefix", "sample"),
        [((chip * CORES + core) * DEPTH + z, (chip * CORES + core) * DEPTH + (z + (1 - 2 * core) * DISTANCE_OF[chip]) % DEPTH)
         for chip in range(PLANE) for core in range(CORES) for z in range(DEPTH)])
    got = lax.ppermute(held, "prefix", [(i, i ^ 1) for i in range(CORES * PLANE)])
    same_core = [[chip * CORES + core for chip in range(PLANE)] for core in range(CORES)]
    copies = pl.pallas_call(
        copy_kernel,
        out_shape=jax.ShapeDtypeStruct((PLANE, ROWS, HD), BF16),
        in_specs=[VMEM],
        out_specs=VMEM,
        compiler_params=budget(2),
        cost_estimate=pl.CostEstimate(flops=10**11, transcendentals=0, bytes_accessed=MIB),
        name="copies",
    )(shifted)
    every_query = lax.all_to_all(copies, "prefix", 0, 0, axis_index_groups=same_core)
    chip_of = jnp.array([CHIP_OF[distance] for distance in range(DEPTH)], jnp.int32)
    partial = pl.pallas_call(
        attend_kernel,
        out_shape=jax.ShapeDtypeStruct((PLANE, BLOCK_ROWS, HD), BF16),
        in_specs=[SMEM, SMEM, SMEM, VMEM, VMEM, VMEM],
        out_specs=VMEM,
        scratch_shapes=[
            pltpu.VMEM((2 * OWN, KVH, HEAD_ROWS, PAGE), F32),
            pltpu.VMEM((2, KVH, 16, PAGE), F32),
        ] + [pltpu.VMEM((PROMPTS + 1, HEAD_ROWS, HD), F32)] * (4 * KVH),
        compiler_params=budget(18),
        name="attend",
    )(page_prompt, suffix_len, chip_of, every_query, held, got)
    partial = lax.all_to_all(partial, "prefix", 0, 0, axis_index_groups=same_core)
    summed = pl.pallas_call(
        plane_kernel,
        out_shape=jax.ShapeDtypeStruct((DEPTH, 16, HD), BF16),
        in_specs=[VMEM],
        out_specs=VMEM,
        compiler_params=budget(4),
        name="plane",
    )(partial)
    summed = lax.all_to_all(summed, "sample", 0, 0)
    return pl.pallas_call(
        final_kernel,
        out_shape=jax.ShapeDtypeStruct((OWN, 2 * HD), BF16),
        in_specs=[VMEM],
        out_specs=VMEM,
        compiler_params=budget(2),
        name="final",
    )(summed)


def solution(mesh):
    placed = (
        P("sample", None),
        P(("prefix", "sample"), None, None),
        P(("prefix", "sample"), None, None),
        P(("prefix", "sample")),
        P("sample", "prefix", None),
        P("sample", "prefix", None),
        P("sample"),
    )
    return jax.shard_map(
        body, mesh=mesh, in_specs=placed, out_specs=P("sample", "prefix"), check_vma=False
    )
```

```python
import functools
import math

import jax
import jax.numpy as jnp
from jax import lax
from jax.experimental import pallas as pl
from jax.experimental.pallas import tpu as pltpu
from jax.sharding import PartitionSpec as P

H = 64
KVH = 8
HD = 128
PAGE = 128
SPP = 16
PROMPTS = 4
CORES = 2
OWN = 4
SPAN = 32
PLANE = 16
DEPTH = 16
ROWS = 128
HEAD_ROWS = 64
STAT_ROWS = 16
BLOCK_ROWS = ROWS + STAT_ROWS
KEY_ROW = 0
VALUE_ROW = PAGE
SUFFIX_KEY_ROW = 2 * PAGE
SUFFIX_VALUE_ROW = 2 * PAGE + SPAN
MARK_ROW = 2 * PAGE + 2 * SPAN
SEND_ROWS = MARK_ROW + 16
NEG = -1e30
MIB = 1 << 20
SCALE = math.log2(math.e) / math.sqrt(HD)
CHIP_ORDER = (0, 4, 1, 2, 8, 3, 12, 5, 6, 9, 13, 7, 14, 11, 10, 15)
DISTANCES = (8, 7, 9, 6, 10, 5, 11, 4, 12, 3, 13, 2, 14, 1, 15, 0)
DISTANCE_OF = dict(zip(CHIP_ORDER, DISTANCES))
CHIP_OF = dict(zip(DISTANCES, CHIP_ORDER))
F32 = jnp.float32
BF16 = jnp.bfloat16


def query_kernel(queries_hbm, out, queries, sem):
    copy = pltpu.make_async_copy(queries_hbm, queries, sem)
    copy.start()
    copy.wait()
    core = lax.rem(lax.axis_index("prefix"), CORES)
    for a in range(KVH):
        parts = []
        for half in range(2):
            for mate in range(2):
                head = a * 8 + half * 4 + mate
                column = pl.multiple_of(head * HD + core * (2 * HD), HD)
                parts.append(queries[:, pl.ds(column, HD)].astype(F32))
        out[pl.ds(a * 16, 16), :] = jnp.concatenate(parts, axis=0).astype(BF16)


def copy_kernel(shifted, out):
    rows = shifted[...]
    for chip in range(PLANE):
        out[chip] = rows


def stage_kernel(page_prompt, pool_keys, pool_values, suffix_keys, suffix_values, out,
                 keys, suffix, prompts, sems):
    pieces = ((page_prompt, prompts), (pool_keys, keys), (suffix_keys, suffix),
              (pool_values, out.at[:, pl.ds(VALUE_ROW, PAGE), :]),
              (suffix_values, out.at[:, pl.ds(SUFFIX_VALUE_ROW, SPAN), :]))
    copies = [pltpu.make_async_copy(src, dst, sems.at[i]) for i, (src, dst) in enumerate(pieces)]
    for copy in copies:
        copy.start()
    copies[0].wait()
    for slot in range(OWN):
        mark = jnp.full((16, KVH * HD), prompts[slot], jnp.int32)
        out[slot, pl.ds(MARK_ROW, 16), :] = mark.astype(F32).astype(BF16)
    copies[1].wait()
    for slot in range(OWN):
        for a in range(KVH):
            head = pl.ds(a * HD, HD)
            out[slot, pl.ds(KEY_ROW, PAGE), head] = keys[slot, :, head].T
    copies[2].wait()
    for a in range(KVH):
        head = pl.ds(a * HD, HD)
        turned = suffix[:, :, head].reshape(OWN * SPAN, HD).T
        out[:, pl.ds(SUFFIX_KEY_ROW, SPAN), head] = turned.reshape(OWN, SPAN, OWN * SPAN)
    for copy in copies[3:]:
        copy.wait()


def attend_kernel(page_prompt, suffix_len, chip_of, queries, held, got, out, scores,
                  suffix_scores, *buffers):
    top, peak, total, acc = (buffers[i * KVH:(i + 1) * KVH] for i in range(4))
    prefix = lax.axis_index("prefix")
    plane = lax.axis_index("sample")
    sign = 1 - 2 * lax.rem(prefix, CORES)
    for a in range(KVH):
        top[a][:PROMPTS] = jnp.full((PROMPTS, HEAD_ROWS, HD), NEG, F32)
        total[a][:PROMPTS] = jnp.zeros((PROMPTS, HEAD_ROWS, HD), F32)
        acc[a][:PROMPTS] = jnp.zeros((PROMPTS, HEAD_ROWS, HD), F32)

    prompts = [page_prompt[slot] for slot in range(OWN)]
    for slot in range(OWN):
        mark = got[slot, pl.ds(MARK_ROW, 16), pl.ds(0, HD)].astype(F32)
        prompts.append(jnp.max(mark).astype(jnp.int32))
    prompts = [jnp.where(prompt >= 0, prompt, PROMPTS) for prompt in prompts]

    own_prompt = lax.div(plane, 4)
    quarter = lax.rem(plane, 4)
    row = lax.broadcasted_iota(jnp.int32, (16, PAGE), 0)
    token = lax.broadcasted_iota(jnp.int32, (16, PAGE), 1)
    token_sample = token >> 5
    length = jnp.where(
        token_sample == 0, suffix_len[0],
        jnp.where(token_sample == 1, suffix_len[1],
                  jnp.where(token_sample == 2, suffix_len[2], suffix_len[3])))
    own_rows = pl.ds(pl.multiple_of(quarter * 16, 16), 16)

    def live(part):
        owner = prefix if part == 0 else prefix + sign
        position = owner * SPAN + (token & (SPAN - 1))
        return ((row & 3) == token_sample) & (position < length)

    def chip_rows(sample_plane, a):
        chip = chip_of[(sign * (plane - sample_plane)) & (DEPTH - 1)]
        return queries[chip, pl.ds(a * 16, 16), :]

    def query_rows(prompt, a):
        return jnp.concatenate([chip_rows(prompt * 4 + q, a) for q in range(4)], axis=0)

    def dot_keys(rows, key):
        return SCALE * lax.dot_general(
            rows, key, (((1,), (0,)), ((), ())), preferred_element_type=F32)

    for part, pages in enumerate((held, got)):
        for slot in range(part * OWN, (part + 1) * OWN):
            for a in range(KVH):
                key = pages[slot % OWN, pl.ds(KEY_ROW, PAGE), pl.ds(a * HD, HD)]
                s = dot_keys(query_rows(prompts[slot], a), key)
                scores[slot, a] = s
                top[a][prompts[slot]] = jnp.maximum(top[a][prompts[slot]], s)

    for part, pages in enumerate((held, got)):
        mask = live(part)
        for a in range(KVH):
            key = pages[:, pl.ds(SUFFIX_KEY_ROW, SPAN), pl.ds(a * HD, HD)]
            key = key.reshape(HD, OWN * SPAN)
            s = jnp.where(mask, dot_keys(chip_rows(plane, a), key), NEG)
            suffix_scores[part, a] = s
            top[a][own_prompt, own_rows] = jnp.maximum(top[a][own_prompt, own_rows], s)

    for a in range(KVH):
        for prompt in range(PROMPTS):
            best = jnp.max(top[a][prompt], axis=1, keepdims=True)
            best = best.astype(BF16).astype(F32)
            peak[a][prompt] = jnp.broadcast_to(best, (HEAD_ROWS, HD))

    for part, pages in enumerate((held, got)):
        for slot in range(part * OWN, (part + 1) * OWN):
            prompt = prompts[slot]
            for a in range(KVH):
                value = pages[slot % OWN, pl.ds(VALUE_ROW, PAGE), pl.ds(a * HD, HD)]
                w = jnp.exp2(scores[slot, a] - peak[a][prompt])
                total[a][prompt] += w
                acc[a][prompt] += jnp.dot(w.astype(BF16), value, preferred_element_type=F32)

    for part, pages in enumerate((held, got)):
        mask = live(part)
        for a in range(KVH):
            value = pages[:, pl.ds(SUFFIX_VALUE_ROW, SPAN), pl.ds(a * HD, HD)]
            value = value.reshape(OWN * SPAN, HD)
            w = jnp.exp2(suffix_scores[part, a] - peak[a][own_prompt, own_rows])
            w = jnp.where(mask, w, 0.0)
            total[a][own_prompt, own_rows] += w
            acc[a][own_prompt, own_rows] += jnp.dot(
                w.astype(BF16), value, preferred_element_type=F32)

    lane = lax.broadcasted_iota(jnp.int32, (HEAD_ROWS, HD), 1)

    for a in range(KVH):
        stats = jnp.zeros((HEAD_ROWS, HD), F32)
        for prompt in range(PROMPTS):
            low = jnp.sum(total[a][prompt], axis=1, keepdims=True)
            high = low.astype(BF16).astype(F32)
            stats = jnp.where(lane == prompt, peak[a][prompt], stats)
            stats = jnp.where(lane == 4 + prompt, high, stats)
            stats = jnp.where(lane == 8 + prompt, low - high, stats)
        for half in range(2):
            def quarter_rows(tile, q):
                return tile[q * 16 + half * 8:q * 16 + half * 8 + 8]
            for prompt in range(PROMPTS):
                sums = acc[a][prompt]
                rows = jnp.concatenate([quarter_rows(sums, q) for q in range(4)], axis=0)
                out[a * 2 + half, pl.ds(prompt * 32, 32), :] = rows.astype(BF16)
            packed = jnp.concatenate(
                [quarter_rows(stats, q) + pltpu.roll(quarter_rows(stats, q + 1), 16, 1)
                 for q in (0, 2)], axis=0)
            out[a * 2 + half, pl.ds(ROWS, STAT_ROWS), :] = packed.astype(BF16)


def tree_sum(terms):
    while len(terms) > 1:
        terms = [a + b for a, b in zip(terms[::2], terms[1::2])]
    return terms[0]


def plane_kernel(got, out):
    stats = [got[src, pl.ds(ROWS, STAT_ROWS), :].astype(F32) for src in range(PLANE)]
    best = functools.reduce(jnp.maximum, stats)
    weights = [jnp.exp2(jnp.minimum(stat - best, 0.0)) for stat in stats]
    def column(tile, prompt, quarter):
        rows, start = quarter // 2 * 8, quarter % 2 * 16 + prompt
        return tile[rows:rows + 8, start:start + 1]

    denominator = tree_sum([
        weight * (pltpu.roll(stat, HD - 4, 1) + pltpu.roll(stat, HD - 8, 1))
        for weight, stat in zip(weights, stats)])
    sums = []
    for prompt in range(PROMPTS):
        tiles = [got[src, pl.ds(prompt * 32, 32), :].astype(F32) for src in range(PLANE)]
        for quarter in range(4):
            rows = slice(quarter * 8, quarter * 8 + 8)
            sums.append(tree_sum([tile[rows] * column(weight, prompt, quarter)
                                  for tile, weight in zip(tiles, weights)]))
    high = denominator.astype(BF16).astype(F32)
    lane = lax.broadcasted_iota(jnp.int32, (8, HD), 1)
    for prompt in range(PROMPTS):
        for quarter in range(4):
            i = prompt * 4 + quarter
            stat = jnp.where(
                lane == 0, column(best, prompt, quarter),
                jnp.where(lane == 1, column(high, prompt, quarter),
                          column(denominator - high, prompt, quarter)))
            out[i] = jnp.concatenate([sums[i], stat], axis=0).astype(BF16)


def final_kernel(got, out):
    tiles = [got[src].astype(F32) for src in range(DEPTH)]
    best = tiles[0][8:16]
    for src in range(1, DEPTH):
        best = jnp.maximum(best, tiles[src][8:16])
    best = best[:, 0:1]
    denominator = jnp.zeros((8, 1), F32)
    numerator = jnp.zeros((8, HD), F32)
    for tile in tiles:
        stat = tile[8:16]
        weight = jnp.exp2(stat[:, 0:1] - best)
        denominator = denominator + weight * (stat[:, 1:2] + stat[:, 2:3])
        numerator = numerator + weight * tile[0:8]
    mixed = (numerator / denominator).astype(BF16)
    out[...] = jnp.concatenate([mixed[0:4], mixed[4:8]], axis=1)


SMEM = pl.BlockSpec(memory_space=pltpu.SMEM)
VMEM = pl.BlockSpec(memory_space=pltpu.VMEM)
ANY = pl.BlockSpec(memory_space=pl.ANY)


def budget(mib):
    return pltpu.CompilerParams(vmem_limit_bytes=int(mib * MIB))


def body(queries, pool_keys, pool_values, page_prompt, suffix_keys, suffix_values, suffix_len):
    own_queries = pl.pallas_call(
        query_kernel,
        out_shape=jax.ShapeDtypeStruct((ROWS, HD), BF16),
        in_specs=[ANY],
        out_specs=VMEM,
        scratch_shapes=[pltpu.VMEM((OWN, H * HD), BF16), pltpu.SemaphoreType.DMA],
        compiler_params=budget(2),
        name="query",
    )(pltpu.with_memory_space_constraint(queries, pltpu.HBM))
    held = pl.pallas_call(
        stage_kernel,
        out_shape=jax.ShapeDtypeStruct((OWN, SEND_ROWS, KVH * HD), BF16),
        in_specs=[ANY] * 5,
        out_specs=VMEM,
        scratch_shapes=[
            pltpu.VMEM((OWN, PAGE, KVH * HD), BF16),
            pltpu.VMEM((OWN, SPAN, KVH * HD), BF16),
            pltpu.SMEM((OWN,), jnp.int32),
            pltpu.SemaphoreType.DMA((5,)),
        ],
        compiler_params=budget(6),
        name="stage",
    )(*(pltpu.with_memory_space_constraint(array, pltpu.HBM)
        for array in (page_prompt, pool_keys, pool_values, suffix_keys, suffix_values)))
    shifted = lax.ppermute(
        own_queries, ("prefix", "sample"),
        [((chip * CORES + core) * DEPTH + z, (chip * CORES + core) * DEPTH + (z + (1 - 2 * core) * DISTANCE_OF[chip]) % DEPTH)
         for chip in range(PLANE) for core in range(CORES) for z in range(DEPTH)])
    got = lax.ppermute(held, "prefix", [(i, i ^ 1) for i in range(CORES * PLANE)])
    same_core = [[chip * CORES + core for chip in range(PLANE)] for core in range(CORES)]
    copies = pl.pallas_call(
        copy_kernel,
        out_shape=jax.ShapeDtypeStruct((PLANE, ROWS, HD), BF16),
        in_specs=[VMEM],
        out_specs=VMEM,
        compiler_params=budget(2),
        cost_estimate=pl.CostEstimate(flops=10**11, transcendentals=0, bytes_accessed=MIB),
        name="copies",
    )(shifted)
    every_query = lax.all_to_all(copies, "prefix", 0, 0, axis_index_groups=same_core)
    chip_of = jnp.array([CHIP_OF[distance] for distance in range(DEPTH)], jnp.int32)
    partial = pl.pallas_call(
        attend_kernel,
        out_shape=jax.ShapeDtypeStruct((PLANE, BLOCK_ROWS, HD), BF16),
        in_specs=[SMEM, SMEM, SMEM, VMEM, VMEM, VMEM],
        out_specs=VMEM,
        scratch_shapes=[
            pltpu.VMEM((2 * OWN, KVH, HEAD_ROWS, PAGE), F32),
            pltpu.VMEM((2, KVH, 16, PAGE), F32),
        ] + [pltpu.VMEM((PROMPTS + 1, HEAD_ROWS, HD), F32)] * (4 * KVH),
        compiler_params=budget(18),
        name="attend",
    )(page_prompt, suffix_len, chip_of, every_query, held, got)
    partial = lax.all_to_all(partial, "prefix", 0, 0, axis_index_groups=same_core)
    summed = pl.pallas_call(
        plane_kernel,
        out_shape=jax.ShapeDtypeStruct((DEPTH, 16, HD), BF16),
        in_specs=[VMEM],
        out_specs=VMEM,
        compiler_params=budget(4),
        name="plane",
    )(partial)
    summed = lax.all_to_all(summed, "sample", 0, 0)
    return pl.pallas_call(
        final_kernel,
        out_shape=jax.ShapeDtypeStruct((OWN, 2 * HD), BF16),
        in_specs=[VMEM],
        out_specs=VMEM,
        compiler_params=budget(2),
        name="final",
    )(summed)


def solution(mesh):
    placed = (
        P("sample", None),
        P(("prefix", "sample"), None, None),
        P(("prefix", "sample"), None, None),
        P(("prefix", "sample")),
        P("sample", "prefix", None),
        P("sample", "prefix", None),
        P("sample"),
    )
    return jax.shard_map(
        body, mesh=mesh, in_specs=placed, out_specs=P("sample", "prefix"), check_vma=False
    )
```

```python
import functools
import math

import jax
import jax.numpy as jnp
from jax import lax
from jax.experimental import pallas as pl
from jax.experimental.pallas import tpu as pltpu
from jax.sharding import PartitionSpec as P

H = 64
KVH = 8
HD = 128
PAGE = 128
SPP = 16
PROMPTS = 4
CORES = 2
OWN = 4
SPAN = 32
PLANE = 16
DEPTH = 16
ROWS = 128
HEAD_ROWS = 64
STAT_ROWS = 16
BLOCK_ROWS = ROWS + STAT_ROWS
KEY_ROW = 0
VALUE_ROW = PAGE
SUFFIX_KEY_ROW = 2 * PAGE
SUFFIX_VALUE_ROW = 2 * PAGE + SPAN
MARK_ROW = 2 * PAGE + 2 * SPAN
SEND_ROWS = MARK_ROW + 16
NEG = -1e30
MIB = 1 << 20
SCALE = math.log2(math.e) / math.sqrt(HD)
CHIP_ORDER = (0, 4, 1, 2, 8, 3, 12, 5, 6, 9, 13, 7, 14, 11, 10, 15)
DISTANCES = (8, 7, 9, 6, 10, 5, 11, 4, 12, 3, 13, 2, 14, 1, 15, 0)
DISTANCE_OF = dict(zip(CHIP_ORDER, DISTANCES))
CHIP_GROUP = tuple(range(10, PLANE)) + tuple(range(10))
PLANE_GROUP = tuple(range(8, DEPTH)) + tuple(range(8))
QUERY_GROUP = tuple(range(0, PLANE)) + tuple(range(0))
CHIP_OF = {distance: QUERY_GROUP.index(chip) for distance, chip in zip(DISTANCES, CHIP_ORDER)}
F32 = jnp.float32
BF16 = jnp.bfloat16


def query_kernel(queries_hbm, out, queries, sem):
    copy = pltpu.make_async_copy(queries_hbm, queries, sem)
    copy.start()
    copy.wait()
    core = lax.rem(lax.axis_index("prefix"), CORES)
    for a in range(KVH):
        parts = []
        for half in range(2):
            for mate in range(2):
                head = a * 8 + half * 4 + mate
                column = pl.multiple_of(head * HD + core * (2 * HD), HD)
                parts.append(queries[:, pl.ds(column, HD)].astype(F32))
        out[pl.ds(a * 16, 16), :] = jnp.concatenate(parts, axis=0).astype(BF16)


def copy_kernel(shifted, out):
    rows = shifted[...]
    for chip in range(PLANE):
        out[chip] = rows


def stage_kernel(page_prompt, pool_keys, pool_values, suffix_keys, suffix_values, out,
                 keys, suffix, prompts, sems):
    pieces = ((page_prompt, prompts), (pool_keys, keys), (suffix_keys, suffix),
              (pool_values, out.at[:, pl.ds(VALUE_ROW, PAGE), :]),
              (suffix_values, out.at[:, pl.ds(SUFFIX_VALUE_ROW, SPAN), :]))
    copies = [pltpu.make_async_copy(src, dst, sems.at[i]) for i, (src, dst) in enumerate(pieces)]
    for copy in copies:
        copy.start()
    copies[0].wait()
    for slot in range(OWN):
        mark = jnp.full((16, KVH * HD), prompts[slot], jnp.int32)
        out[slot, pl.ds(MARK_ROW, 16), :] = mark.astype(F32).astype(BF16)
    copies[1].wait()
    for slot in range(OWN):
        for a in range(KVH):
            head = pl.ds(a * HD, HD)
            out[slot, pl.ds(KEY_ROW, PAGE), head] = keys[slot, :, head].T
    copies[2].wait()
    for a in range(KVH):
        head = pl.ds(a * HD, HD)
        turned = suffix[:, :, head].reshape(OWN * SPAN, HD).T
        out[:, pl.ds(SUFFIX_KEY_ROW, SPAN), head] = turned.reshape(OWN, SPAN, OWN * SPAN)
    for copy in copies[3:]:
        copy.wait()


def attend_kernel(page_prompt, suffix_len, chip_of, queries, held, got, out, scores,
                  suffix_scores, *buffers):
    top, peak, total, acc = (buffers[i * KVH:(i + 1) * KVH] for i in range(4))
    prefix = lax.axis_index("prefix")
    plane = lax.axis_index("sample")
    sign = 1 - 2 * lax.rem(prefix, CORES)
    for a in range(KVH):
        top[a][:PROMPTS] = jnp.full((PROMPTS, HEAD_ROWS, HD), NEG, F32)
        total[a][:PROMPTS] = jnp.zeros((PROMPTS, HEAD_ROWS, HD), F32)
        acc[a][:PROMPTS] = jnp.zeros((PROMPTS, HEAD_ROWS, HD), F32)

    prompts = [page_prompt[slot] for slot in range(OWN)]
    for slot in range(OWN):
        mark = got[slot, pl.ds(MARK_ROW, 16), pl.ds(0, HD)].astype(F32)
        prompts.append(jnp.max(mark).astype(jnp.int32))
    prompts = [jnp.where(prompt >= 0, prompt, PROMPTS) for prompt in prompts]

    own_prompt = lax.div(plane, 4)
    quarter = lax.rem(plane, 4)
    row = lax.broadcasted_iota(jnp.int32, (16, PAGE), 0)
    token = lax.broadcasted_iota(jnp.int32, (16, PAGE), 1)
    token_sample = token >> 5
    length = jnp.where(
        token_sample == 0, suffix_len[0],
        jnp.where(token_sample == 1, suffix_len[1],
                  jnp.where(token_sample == 2, suffix_len[2], suffix_len[3])))
    own_rows = pl.ds(pl.multiple_of(quarter * 16, 16), 16)

    def live(part):
        owner = prefix if part == 0 else prefix + sign
        position = owner * SPAN + (token & (SPAN - 1))
        return ((row & 3) == token_sample) & (position < length)

    def chip_rows(sample_plane, a):
        chip = chip_of[(sign * (plane - sample_plane)) & (DEPTH - 1)]
        return queries[chip, pl.ds(a * 16, 16), :]

    def query_rows(prompt, a):
        return jnp.concatenate([chip_rows(prompt * 4 + q, a) for q in range(4)], axis=0)

    def dot_keys(rows, key):
        return SCALE * lax.dot_general(
            rows, key, (((1,), (0,)), ((), ())), preferred_element_type=F32)

    for part, pages in enumerate((held, got)):
        for slot in range(part * OWN, (part + 1) * OWN):
            for a in range(KVH):
                key = pages[slot % OWN, pl.ds(KEY_ROW, PAGE), pl.ds(a * HD, HD)]
                s = dot_keys(query_rows(prompts[slot], a), key)
                scores[slot, a] = s
                top[a][prompts[slot]] = jnp.maximum(top[a][prompts[slot]], s)

    for part, pages in enumerate((held, got)):
        mask = live(part)
        for a in range(KVH):
            key = pages[:, pl.ds(SUFFIX_KEY_ROW, SPAN), pl.ds(a * HD, HD)]
            key = key.reshape(HD, OWN * SPAN)
            s = jnp.where(mask, dot_keys(chip_rows(plane, a), key), NEG)
            suffix_scores[part, a] = s
            top[a][own_prompt, own_rows] = jnp.maximum(top[a][own_prompt, own_rows], s)

    for a in range(KVH):
        for prompt in range(PROMPTS):
            best = jnp.max(top[a][prompt], axis=1, keepdims=True)
            best = best.astype(BF16).astype(F32)
            peak[a][prompt] = jnp.broadcast_to(best, (HEAD_ROWS, HD))

    for part, pages in enumerate((held, got)):
        for slot in range(part * OWN, (part + 1) * OWN):
            prompt = prompts[slot]
            for a in range(KVH):
                value = pages[slot % OWN, pl.ds(VALUE_ROW, PAGE), pl.ds(a * HD, HD)]
                w = jnp.exp2(scores[slot, a] - peak[a][prompt])
                total[a][prompt] += w
                acc[a][prompt] += jnp.dot(w.astype(BF16), value, preferred_element_type=F32)

    for part, pages in enumerate((held, got)):
        mask = live(part)
        for a in range(KVH):
            value = pages[:, pl.ds(SUFFIX_VALUE_ROW, SPAN), pl.ds(a * HD, HD)]
            value = value.reshape(OWN * SPAN, HD)
            w = jnp.exp2(suffix_scores[part, a] - peak[a][own_prompt, own_rows])
            w = jnp.where(mask, w, 0.0)
            total[a][own_prompt, own_rows] += w
            acc[a][own_prompt, own_rows] += jnp.dot(
                w.astype(BF16), value, preferred_element_type=F32)

    lane = lax.broadcasted_iota(jnp.int32, (HEAD_ROWS, HD), 1)

    for a in range(KVH):
        stats = jnp.zeros((HEAD_ROWS, HD), F32)
        for prompt in range(PROMPTS):
            low = jnp.sum(total[a][prompt], axis=1, keepdims=True)
            high = low.astype(BF16).astype(F32)
            stats = jnp.where(lane == prompt, peak[a][prompt], stats)
            stats = jnp.where(lane == 4 + prompt, high, stats)
            stats = jnp.where(lane == 8 + prompt, low - high, stats)
        for half in range(2):
            def quarter_rows(tile, q):
                return tile[q * 16 + half * 8:q * 16 + half * 8 + 8]
            owner = CHIP_GROUP.index(a * 2 + half)
            for prompt in range(PROMPTS):
                sums = acc[a][prompt]
                rows = jnp.concatenate([quarter_rows(sums, q) for q in range(4)], axis=0)
                out[owner, pl.ds(prompt * 32, 32), :] = rows.astype(BF16)
            packed = jnp.concatenate(
                [quarter_rows(stats, q) + pltpu.roll(quarter_rows(stats, q + 1), 16, 1)
                 for q in (0, 2)], axis=0)
            out[owner, pl.ds(ROWS, STAT_ROWS), :] = packed.astype(BF16)


def tree_sum(terms):
    while len(terms) > 1:
        terms = [a + b for a, b in zip(terms[::2], terms[1::2])]
    return terms[0]


def plane_kernel(got, out):
    stats = [got[src, pl.ds(ROWS, STAT_ROWS), :].astype(F32) for src in range(PLANE)]
    best = functools.reduce(jnp.maximum, stats)
    weights = [jnp.exp2(jnp.minimum(stat - best, 0.0)) for stat in stats]
    def column(tile, prompt, quarter):
        rows, start = quarter // 2 * 8, quarter % 2 * 16 + prompt
        return tile[rows:rows + 8, start:start + 1]

    denominator = tree_sum([
        weight * (pltpu.roll(stat, HD - 4, 1) + pltpu.roll(stat, HD - 8, 1))
        for weight, stat in zip(weights, stats)])
    sums = []
    for prompt in range(PROMPTS):
        tiles = [got[src, pl.ds(prompt * 32, 32), :].astype(F32) for src in range(PLANE)]
        for quarter in range(4):
            rows = slice(quarter * 8, quarter * 8 + 8)
            sums.append(tree_sum([tile[rows] * column(weight, prompt, quarter)
                                  for tile, weight in zip(tiles, weights)]))
    high = denominator.astype(BF16).astype(F32)
    lane = lax.broadcasted_iota(jnp.int32, (8, HD), 1)
    for prompt in range(PROMPTS):
        for quarter in range(4):
            i = prompt * 4 + quarter
            stat = jnp.where(
                lane == 0, column(best, prompt, quarter),
                jnp.where(lane == 1, column(high, prompt, quarter),
                          column(denominator - high, prompt, quarter)))
            out[PLANE_GROUP.index(i)] = jnp.concatenate([sums[i], stat], axis=0).astype(BF16)


def final_kernel(got, out):
    tiles = [got[src].astype(F32) for src in range(DEPTH)]
    best = tiles[0][8:16]
    for src in range(1, DEPTH):
        best = jnp.maximum(best, tiles[src][8:16])
    best = best[:, 0:1]
    denominator = jnp.zeros((8, 1), F32)
    numerator = jnp.zeros((8, HD), F32)
    for tile in tiles:
        stat = tile[8:16]
        weight = jnp.exp2(stat[:, 0:1] - best)
        denominator = denominator + weight * (stat[:, 1:2] + stat[:, 2:3])
        numerator = numerator + weight * tile[0:8]
    mixed = (numerator / denominator).astype(BF16)
    out[...] = jnp.concatenate([mixed[0:4], mixed[4:8]], axis=1)


SMEM = pl.BlockSpec(memory_space=pltpu.SMEM)
VMEM = pl.BlockSpec(memory_space=pltpu.VMEM)
ANY = pl.BlockSpec(memory_space=pl.ANY)


def budget(mib):
    return pltpu.CompilerParams(vmem_limit_bytes=int(mib * MIB))


def body(queries, pool_keys, pool_values, page_prompt, suffix_keys, suffix_values, suffix_len):
    own_queries = pl.pallas_call(
        query_kernel,
        out_shape=jax.ShapeDtypeStruct((ROWS, HD), BF16),
        in_specs=[ANY],
        out_specs=VMEM,
        scratch_shapes=[pltpu.VMEM((OWN, H * HD), BF16), pltpu.SemaphoreType.DMA],
        compiler_params=budget(2),
        name="query",
    )(pltpu.with_memory_space_constraint(queries, pltpu.HBM))
    held = pl.pallas_call(
        stage_kernel,
        out_shape=jax.ShapeDtypeStruct((OWN, SEND_ROWS, KVH * HD), BF16),
        in_specs=[ANY] * 5,
        out_specs=VMEM,
        scratch_shapes=[
            pltpu.VMEM((OWN, PAGE, KVH * HD), BF16),
            pltpu.VMEM((OWN, SPAN, KVH * HD), BF16),
            pltpu.SMEM((OWN,), jnp.int32),
            pltpu.SemaphoreType.DMA((5,)),
        ],
        compiler_params=budget(6),
        name="stage",
    )(*(pltpu.with_memory_space_constraint(array, pltpu.HBM)
        for array in (page_prompt, pool_keys, pool_values, suffix_keys, suffix_values)))
    shifted = lax.ppermute(
        own_queries, ("prefix", "sample"),
        [((chip * CORES + core) * DEPTH + z, (chip * CORES + core) * DEPTH + (z + (1 - 2 * core) * DISTANCE_OF[chip]) % DEPTH)
         for chip in range(PLANE) for core in range(CORES) for z in range(DEPTH)])
    got = lax.ppermute(held, "prefix", [(i, i ^ 1) for i in range(CORES * PLANE)])
    same_core = [[chip * CORES + core for chip in CHIP_GROUP] for core in range(CORES)]
    copies = pl.pallas_call(
        copy_kernel,
        out_shape=jax.ShapeDtypeStruct((PLANE, ROWS, HD), BF16),
        in_specs=[VMEM],
        out_specs=VMEM,
        compiler_params=budget(2),
        cost_estimate=pl.CostEstimate(flops=10**11, transcendentals=0, bytes_accessed=MIB),
        name="copies",
    )(shifted)
    every_query = lax.all_to_all(
        copies, "prefix", 0, 0,
        axis_index_groups=[[chip * CORES + core for chip in QUERY_GROUP] for core in range(CORES)])
    chip_of = jnp.array([CHIP_OF[distance] for distance in range(DEPTH)], jnp.int32)
    partial = pl.pallas_call(
        attend_kernel,
        out_shape=jax.ShapeDtypeStruct((PLANE, BLOCK_ROWS, HD), BF16),
        in_specs=[SMEM, SMEM, SMEM, VMEM, VMEM, VMEM],
        out_specs=VMEM,
        scratch_shapes=[
            pltpu.VMEM((2 * OWN, KVH, HEAD_ROWS, PAGE), F32),
            pltpu.VMEM((2, KVH, 16, PAGE), F32),
        ] + [pltpu.VMEM((PROMPTS + 1, HEAD_ROWS, HD), F32)] * (4 * KVH),
        compiler_params=budget(18),
        name="attend",
    )(page_prompt, suffix_len, chip_of, every_query, held, got)
    partial = lax.all_to_all(partial, "prefix", 0, 0, axis_index_groups=same_core)
    summed = pl.pallas_call(
        plane_kernel,
        out_shape=jax.ShapeDtypeStruct((DEPTH, 16, HD), BF16),
        in_specs=[VMEM],
        out_specs=VMEM,
        compiler_params=budget(4),
        name="plane",
    )(partial)
    summed = lax.all_to_all(summed, "sample", 0, 0, axis_index_groups=[list(PLANE_GROUP)])
    return pl.pallas_call(
        final_kernel,
        out_shape=jax.ShapeDtypeStruct((OWN, 2 * HD), BF16),
        in_specs=[VMEM],
        out_specs=VMEM,
        compiler_params=budget(2),
        name="final",
    )(summed)


def solution(mesh):
    placed = (
        P("sample", None),
        P(("prefix", "sample"), None, None),
        P(("prefix", "sample"), None, None),
        P(("prefix", "sample")),
        P("sample", "prefix", None),
        P("sample", "prefix", None),
        P("sample"),
    )
    return jax.shard_map(
        body, mesh=mesh, in_specs=placed, out_specs=P("sample", "prefix"), check_vma=False
    )
```

```python
import functools
import math

import jax
import jax.numpy as jnp
from jax import lax
from jax.experimental import pallas as pl
from jax.experimental.pallas import tpu as pltpu
from jax.sharding import PartitionSpec as P

H = 64
KVH = 8
HD = 128
PAGE = 128
SPP = 16
PROMPTS = 4
CORES = 2
OWN = 4
SPAN = 32
PLANE = 16
DEPTH = 16
ROWS = 128
HEAD_ROWS = 64
STAT_ROWS = 16
BLOCK_ROWS = ROWS + STAT_ROWS
KEY_ROW = 0
VALUE_ROW = PAGE
SUFFIX_KEY_ROW = 2 * PAGE
SUFFIX_VALUE_ROW = 2 * PAGE + SPAN
MARK_ROW = 2 * PAGE + 2 * SPAN
SEND_ROWS = MARK_ROW + 16
NEG = -1e30
MIB = 1 << 20
SCALE = math.log2(math.e) / math.sqrt(HD)
CHIP_ORDER = (0, 4, 1, 2, 8, 3, 12, 5, 6, 9, 13, 7, 14, 11, 10, 15)
DISTANCES = (8, 7, 9, 6, 10, 5, 11, 4, 12, 3, 13, 2, 14, 1, 15, 0)
DISTANCE_OF = dict(zip(CHIP_ORDER, DISTANCES))
CHIP_GROUP = tuple(range(10, PLANE)) + tuple(range(10))
PLANE_GROUP = tuple(range(8, DEPTH)) + tuple(range(8))
QUERY_GROUP = tuple(range(1, PLANE)) + tuple(range(1))
CHIP_OF = {distance: QUERY_GROUP.index(chip) for distance, chip in zip(DISTANCES, CHIP_ORDER)}
EARLY_PLANES = 7
F32 = jnp.float32
BF16 = jnp.bfloat16


def stage(page_prompt, pool_keys, pool_values, suffix_keys, suffix_values, out,
          keys, suffix, prompts, sems):
    pieces = ((page_prompt, prompts), (pool_keys, keys), (suffix_keys, suffix),
              (pool_values, out.at[:, pl.ds(VALUE_ROW, PAGE), :]),
              (suffix_values, out.at[:, pl.ds(SUFFIX_VALUE_ROW, SPAN), :]))
    copies = [pltpu.make_async_copy(src, dst, sems.at[i]) for i, (src, dst) in enumerate(pieces)]
    for copy in copies:
        copy.start()
    copies[0].wait()
    for slot in range(OWN):
        mark = jnp.full((16, KVH * HD), prompts[slot], jnp.int32)
        out[slot, pl.ds(MARK_ROW, 16), :] = mark.astype(F32).astype(BF16)
    copies[1].wait()
    for slot in range(OWN):
        for a in range(KVH):
            head = pl.ds(a * HD, HD)
            out[slot, pl.ds(KEY_ROW, PAGE), head] = keys[slot, :, head].T
    copies[2].wait()
    for a in range(KVH):
        head = pl.ds(a * HD, HD)
        turned = suffix[:, :, head].reshape(OWN * SPAN, HD).T
        out[:, pl.ds(SUFFIX_KEY_ROW, SPAN), head] = turned.reshape(OWN, SPAN, OWN * SPAN)
    for copy in copies[3:]:
        copy.wait()


def query_kernel(queries_hbm, page_prompt, pool_keys, pool_values, suffix_keys, suffix_values,
                 out, held, queries, sem, *scratch):
    copy = pltpu.make_async_copy(queries_hbm, queries, sem)
    copy.start()
    copy.wait()
    core = lax.rem(lax.axis_index("prefix"), CORES)
    for a in range(KVH):
        parts = []
        for half in range(2):
            for mate in range(2):
                head = a * 8 + half * 4 + mate
                column = pl.multiple_of(head * HD + core * (2 * HD), HD)
                parts.append(queries[:, pl.ds(column, HD)].astype(F32))
        out[pl.ds(a * 16, 16), :] = jnp.concatenate(parts, axis=0).astype(BF16)

    @pl.when(lax.axis_index("sample") < EARLY_PLANES)
    def _():
        stage(page_prompt, pool_keys, pool_values, suffix_keys, suffix_values, held, *scratch)


def stage_kernel(page_prompt, pool_keys, pool_values, suffix_keys, suffix_values, held, out,
                 *scratch):
    @pl.when(lax.axis_index("sample") >= EARLY_PLANES)
    def _():
        stage(page_prompt, pool_keys, pool_values, suffix_keys, suffix_values, out, *scratch)


def copy_kernel(shifted, out):
    rows = shifted[...]
    for chip in range(PLANE):
        out[chip] = rows


def attend_kernel(page_prompt, suffix_len, chip_of, queries, held, got, out, scores,
                  suffix_scores, *buffers):
    top, peak, total, acc = (buffers[i * KVH:(i + 1) * KVH] for i in range(4))
    prefix = lax.axis_index("prefix")
    plane = lax.axis_index("sample")
    sign = 1 - 2 * lax.rem(prefix, CORES)
    for a in range(KVH):
        top[a][:PROMPTS] = jnp.full((PROMPTS, HEAD_ROWS, HD), NEG, F32)
        total[a][:PROMPTS] = jnp.zeros((PROMPTS, HEAD_ROWS, HD), F32)
        acc[a][:PROMPTS] = jnp.zeros((PROMPTS, HEAD_ROWS, HD), F32)

    prompts = [page_prompt[slot] for slot in range(OWN)]
    for slot in range(OWN):
        mark = got[slot, pl.ds(MARK_ROW, 16), pl.ds(0, HD)].astype(F32)
        prompts.append(jnp.max(mark).astype(jnp.int32))
    prompts = [jnp.where(prompt >= 0, prompt, PROMPTS) for prompt in prompts]

    own_prompt = lax.div(plane, 4)
    quarter = lax.rem(plane, 4)
    row = lax.broadcasted_iota(jnp.int32, (16, PAGE), 0)
    token = lax.broadcasted_iota(jnp.int32, (16, PAGE), 1)
    token_sample = token >> 5
    length = jnp.where(
        token_sample == 0, suffix_len[0],
        jnp.where(token_sample == 1, suffix_len[1],
                  jnp.where(token_sample == 2, suffix_len[2], suffix_len[3])))
    own_rows = pl.ds(pl.multiple_of(quarter * 16, 16), 16)

    def live(part):
        owner = prefix if part == 0 else prefix + sign
        position = owner * SPAN + (token & (SPAN - 1))
        return ((row & 3) == token_sample) & (position < length)

    def chip_rows(sample_plane, a):
        chip = chip_of[(sign * (plane - sample_plane)) & (DEPTH - 1)]
        return queries[chip, pl.ds(a * 16, 16), :]

    def query_rows(prompt, a):
        return jnp.concatenate([chip_rows(prompt * 4 + q, a) for q in range(4)], axis=0)

    def dot_keys(rows, key):
        return SCALE * lax.dot_general(
            rows, key, (((1,), (0,)), ((), ())), preferred_element_type=F32)

    for part, pages in enumerate((held, got)):
        for slot in range(part * OWN, (part + 1) * OWN):
            for a in range(KVH):
                key = pages[slot % OWN, pl.ds(KEY_ROW, PAGE), pl.ds(a * HD, HD)]
                s = dot_keys(query_rows(prompts[slot], a), key)
                scores[slot, a] = s
                top[a][prompts[slot]] = jnp.maximum(top[a][prompts[slot]], s)

    for part, pages in enumerate((held, got)):
        mask = live(part)
        for a in range(KVH):
            key = pages[:, pl.ds(SUFFIX_KEY_ROW, SPAN), pl.ds(a * HD, HD)]
            key = key.reshape(HD, OWN * SPAN)
            s = jnp.where(mask, dot_keys(chip_rows(plane, a), key), NEG)
            suffix_scores[part, a] = s
            top[a][own_prompt, own_rows] = jnp.maximum(top[a][own_prompt, own_rows], s)

    for a in range(KVH):
        for prompt in range(PROMPTS):
            best = jnp.max(top[a][prompt], axis=1, keepdims=True)
            best = best.astype(BF16).astype(F32)
            peak[a][prompt] = jnp.broadcast_to(best, (HEAD_ROWS, HD))

    for part, pages in enumerate((held, got)):
        for slot in range(part * OWN, (part + 1) * OWN):
            prompt = prompts[slot]
            for a in range(KVH):
                value = pages[slot % OWN, pl.ds(VALUE_ROW, PAGE), pl.ds(a * HD, HD)]
                w = jnp.exp2(scores[slot, a] - peak[a][prompt])
                total[a][prompt] += w
                acc[a][prompt] += jnp.dot(w.astype(BF16), value, preferred_element_type=F32)

    for part, pages in enumerate((held, got)):
        mask = live(part)
        for a in range(KVH):
            value = pages[:, pl.ds(SUFFIX_VALUE_ROW, SPAN), pl.ds(a * HD, HD)]
            value = value.reshape(OWN * SPAN, HD)
            w = jnp.exp2(suffix_scores[part, a] - peak[a][own_prompt, own_rows])
            w = jnp.where(mask, w, 0.0)
            total[a][own_prompt, own_rows] += w
            acc[a][own_prompt, own_rows] += jnp.dot(
                w.astype(BF16), value, preferred_element_type=F32)

    lane = lax.broadcasted_iota(jnp.int32, (HEAD_ROWS, HD), 1)

    for a in range(KVH):
        stats = jnp.zeros((HEAD_ROWS, HD), F32)
        for prompt in range(PROMPTS):
            low = jnp.sum(total[a][prompt], axis=1, keepdims=True)
            high = low.astype(BF16).astype(F32)
            stats = jnp.where(lane == prompt, peak[a][prompt], stats)
            stats = jnp.where(lane == 4 + prompt, high, stats)
            stats = jnp.where(lane == 8 + prompt, low - high, stats)
        for half in range(2):
            def quarter_rows(tile, q):
                return tile[q * 16 + half * 8:q * 16 + half * 8 + 8]
            owner = CHIP_GROUP.index(a * 2 + half)
            for prompt in range(PROMPTS):
                sums = acc[a][prompt]
                rows = jnp.concatenate([quarter_rows(sums, q) for q in range(4)], axis=0)
                out[owner, pl.ds(prompt * 32, 32), :] = rows.astype(BF16)
            packed = jnp.concatenate(
                [quarter_rows(stats, q) + pltpu.roll(quarter_rows(stats, q + 1), 16, 1)
                 for q in (0, 2)], axis=0)
            out[owner, pl.ds(ROWS, STAT_ROWS), :] = packed.astype(BF16)


def tree_sum(terms):
    while len(terms) > 1:
        terms = [a + b for a, b in zip(terms[::2], terms[1::2])]
    return terms[0]


def plane_kernel(got, out):
    stats = [got[src, pl.ds(ROWS, STAT_ROWS), :].astype(F32) for src in range(PLANE)]
    best = functools.reduce(jnp.maximum, stats)
    weights = [jnp.exp2(jnp.minimum(stat - best, 0.0)) for stat in stats]
    def column(tile, prompt, quarter):
        rows, start = quarter // 2 * 8, quarter % 2 * 16 + prompt
        return tile[rows:rows + 8, start:start + 1]

    denominator = tree_sum([
        weight * (pltpu.roll(stat, HD - 4, 1) + pltpu.roll(stat, HD - 8, 1))
        for weight, stat in zip(weights, stats)])
    sums = []
    for prompt in range(PROMPTS):
        tiles = [got[src, pl.ds(prompt * 32, 32), :].astype(F32) for src in range(PLANE)]
        for quarter in range(4):
            rows = slice(quarter * 8, quarter * 8 + 8)
            sums.append(tree_sum([tile[rows] * column(weight, prompt, quarter)
                                  for tile, weight in zip(tiles, weights)]))
    high = denominator.astype(BF16).astype(F32)
    lane = lax.broadcasted_iota(jnp.int32, (8, HD), 1)
    for prompt in range(PROMPTS):
        for quarter in range(4):
            i = prompt * 4 + quarter
            stat = jnp.where(
                lane == 0, column(best, prompt, quarter),
                jnp.where(lane == 1, column(high, prompt, quarter),
                          column(denominator - high, prompt, quarter)))
            out[PLANE_GROUP.index(i)] = jnp.concatenate([sums[i], stat], axis=0).astype(BF16)


def final_kernel(got, out):
    tiles = [got[src].astype(F32) for src in range(DEPTH)]
    best = tiles[0][8:16]
    for src in range(1, DEPTH):
        best = jnp.maximum(best, tiles[src][8:16])
    best = best[:, 0:1]
    denominator = jnp.zeros((8, 1), F32)
    numerator = jnp.zeros((8, HD), F32)
    for tile in tiles:
        stat = tile[8:16]
        weight = jnp.exp2(stat[:, 0:1] - best)
        denominator = denominator + weight * (stat[:, 1:2] + stat[:, 2:3])
        numerator = numerator + weight * tile[0:8]
    mixed = (numerator / denominator).astype(BF16)
    out[...] = jnp.concatenate([mixed[0:4], mixed[4:8]], axis=1)


SMEM = pl.BlockSpec(memory_space=pltpu.SMEM)
VMEM = pl.BlockSpec(memory_space=pltpu.VMEM)
ANY = pl.BlockSpec(memory_space=pl.ANY)


def budget(mib):
    return pltpu.CompilerParams(vmem_limit_bytes=int(mib * MIB))


def body(queries, pool_keys, pool_values, page_prompt, suffix_keys, suffix_values, suffix_len):
    def pages():
        return tuple(
            pltpu.with_memory_space_constraint(array, pltpu.HBM)
            for array in (page_prompt, pool_keys, pool_values, suffix_keys, suffix_values))

    room = [
        pltpu.VMEM((OWN, PAGE, KVH * HD), BF16),
        pltpu.VMEM((OWN, SPAN, KVH * HD), BF16),
        pltpu.SMEM((OWN,), jnp.int32),
        pltpu.SemaphoreType.DMA((5,)),
    ]
    held_shape = jax.ShapeDtypeStruct((OWN, SEND_ROWS, KVH * HD), BF16)
    own_queries, held = pl.pallas_call(
        query_kernel,
        out_shape=(jax.ShapeDtypeStruct((ROWS, HD), BF16), held_shape),
        in_specs=[ANY] * 6,
        out_specs=(VMEM, VMEM),
        scratch_shapes=[pltpu.VMEM((OWN, H * HD), BF16), pltpu.SemaphoreType.DMA] + room,
        compiler_params=budget(6),
        name="query",
    )(pltpu.with_memory_space_constraint(queries, pltpu.HBM), *pages())
    held = pl.pallas_call(
        stage_kernel,
        out_shape=held_shape,
        in_specs=[ANY] * 5 + [VMEM],
        out_specs=VMEM,
        input_output_aliases={5: 0},
        scratch_shapes=room,
        compiler_params=budget(6),
        name="stage",
    )(*pages(), held)
    shifted = lax.ppermute(
        own_queries, ("prefix", "sample"),
        [((chip * CORES + core) * DEPTH + z, (chip * CORES + core) * DEPTH + (z + (1 - 2 * core) * DISTANCE_OF[chip]) % DEPTH)
         for chip in range(PLANE) for core in range(CORES) for z in range(DEPTH)])
    got = lax.ppermute(held, "prefix", [(i, i ^ 1) for i in range(CORES * PLANE)])
    same_core = [[chip * CORES + core for chip in CHIP_GROUP] for core in range(CORES)]
    copies = pl.pallas_call(
        copy_kernel,
        out_shape=jax.ShapeDtypeStruct((PLANE, ROWS, HD), BF16),
        in_specs=[VMEM],
        out_specs=VMEM,
        compiler_params=budget(2),
        cost_estimate=pl.CostEstimate(flops=10**11, transcendentals=0, bytes_accessed=MIB),
        name="copies",
    )(shifted)
    every_query = lax.all_to_all(
        copies, "prefix", 0, 0,
        axis_index_groups=[[chip * CORES + core for chip in QUERY_GROUP] for core in range(CORES)])
    chip_of = jnp.array([CHIP_OF[distance] for distance in range(DEPTH)], jnp.int32)
    partial = pl.pallas_call(
        attend_kernel,
        out_shape=jax.ShapeDtypeStruct((PLANE, BLOCK_ROWS, HD), BF16),
        in_specs=[SMEM, SMEM, SMEM, VMEM, VMEM, VMEM],
        out_specs=VMEM,
        scratch_shapes=[
            pltpu.VMEM((2 * OWN, KVH, HEAD_ROWS, PAGE), F32),
            pltpu.VMEM((2, KVH, 16, PAGE), F32),
        ] + [pltpu.VMEM((PROMPTS + 1, HEAD_ROWS, HD), F32)] * (4 * KVH),
        compiler_params=budget(18),
        name="attend",
    )(page_prompt, suffix_len, chip_of, every_query, held, got)
    partial = lax.all_to_all(partial, "prefix", 0, 0, axis_index_groups=same_core)
    summed = pl.pallas_call(
        plane_kernel,
        out_shape=jax.ShapeDtypeStruct((DEPTH, 16, HD), BF16),
        in_specs=[VMEM],
        out_specs=VMEM,
        compiler_params=budget(4),
        name="plane",
    )(partial)
    summed = lax.all_to_all(summed, "sample", 0, 0, axis_index_groups=[list(PLANE_GROUP)])
    return pl.pallas_call(
        final_kernel,
        out_shape=jax.ShapeDtypeStruct((OWN, 2 * HD), BF16),
        in_specs=[VMEM],
        out_specs=VMEM,
        compiler_params=budget(2),
        name="final",
    )(summed)


def solution(mesh):
    placed = (
        P("sample", None),
        P(("prefix", "sample"), None, None),
        P(("prefix", "sample"), None, None),
        P(("prefix", "sample")),
        P("sample", "prefix", None),
        P("sample", "prefix", None),
        P("sample"),
    )
    return jax.shard_map(
        body, mesh=mesh, in_specs=placed, out_specs=P("sample", "prefix"), check_vma=False
    )
```

```python
import functools
import math

import jax
import jax.numpy as jnp
from jax import lax
from jax.experimental import pallas as pl
from jax.experimental.pallas import tpu as pltpu
from jax.sharding import PartitionSpec as P

H = 64
KVH = 8
HD = 128
PAGE = 128
SPP = 16
PROMPTS = 4
CORES = 2
OWN = 4
SPAN = 32
PLANE = 16
DEPTH = 16
ROWS = 128
HEAD_ROWS = 64
STAT_ROWS = 16
BLOCK_ROWS = ROWS + STAT_ROWS
KEY_ROW = 0
VALUE_ROW = PAGE
SUFFIX_KEY_ROW = 2 * PAGE
SUFFIX_VALUE_ROW = 2 * PAGE + SPAN
MARK_ROW = 2 * PAGE + 2 * SPAN
SEND_ROWS = MARK_ROW + 16
NEG = -1e30
MIB = 1 << 20
SCALE = math.log2(math.e) / math.sqrt(HD)
CHIP_ORDER = (0, 4, 1, 2, 8, 3, 12, 5, 6, 9, 13, 7, 14, 11, 10, 15)
DISTANCES = (8, 7, 9, 6, 10, 5, 11, 4, 12, 3, 13, 2, 14, 1, 15, 0)
DISTANCE_OF = dict(zip(CHIP_ORDER, DISTANCES))
SUM_FIRST = (10, 0)
QUERY_FIRST = (1, 11)
PLANE_GROUP = tuple(range(8, DEPTH)) + tuple(range(8))
CHIP_OF = dict(zip(DISTANCES, CHIP_ORDER))
EARLY_PLANES = 7
F32 = jnp.float32
BF16 = jnp.bfloat16


def stage(page_prompt, pool_keys, pool_values, suffix_keys, suffix_values, out,
          keys, suffix, prompts, sems):
    pieces = ((page_prompt, prompts), (pool_keys, keys), (suffix_keys, suffix),
              (pool_values, out.at[:, pl.ds(VALUE_ROW, PAGE), :]),
              (suffix_values, out.at[:, pl.ds(SUFFIX_VALUE_ROW, SPAN), :]))
    copies = [pltpu.make_async_copy(src, dst, sems.at[i]) for i, (src, dst) in enumerate(pieces)]
    for copy in copies:
        copy.start()
    copies[0].wait()
    for slot in range(OWN):
        mark = jnp.full((16, KVH * HD), prompts[slot], jnp.int32)
        out[slot, pl.ds(MARK_ROW, 16), :] = mark.astype(F32).astype(BF16)
    copies[1].wait()
    for slot in range(OWN):
        for a in range(KVH):
            head = pl.ds(a * HD, HD)
            out[slot, pl.ds(KEY_ROW, PAGE), head] = keys[slot, :, head].T
    copies[2].wait()
    for a in range(KVH):
        head = pl.ds(a * HD, HD)
        turned = suffix[:, :, head].reshape(OWN * SPAN, HD).T
        out[:, pl.ds(SUFFIX_KEY_ROW, SPAN), head] = turned.reshape(OWN, SPAN, OWN * SPAN)
    for copy in copies[3:]:
        copy.wait()


def query_kernel(queries_hbm, page_prompt, pool_keys, pool_values, suffix_keys, suffix_values,
                 out, held, queries, sem, *scratch):
    copy = pltpu.make_async_copy(queries_hbm, queries, sem)
    copy.start()
    copy.wait()
    core = lax.rem(lax.axis_index("prefix"), CORES)
    for a in range(KVH):
        parts = []
        for half in range(2):
            for mate in range(2):
                head = a * 8 + half * 4 + mate
                column = pl.multiple_of(head * HD + core * (2 * HD), HD)
                parts.append(queries[:, pl.ds(column, HD)].astype(F32))
        out[pl.ds(a * 16, 16), :] = jnp.concatenate(parts, axis=0).astype(BF16)

    @pl.when(lax.axis_index("sample") < EARLY_PLANES)
    def _():
        stage(page_prompt, pool_keys, pool_values, suffix_keys, suffix_values, held, *scratch)


def stage_kernel(page_prompt, pool_keys, pool_values, suffix_keys, suffix_values, held, out,
                 *scratch):
    @pl.when(lax.axis_index("sample") >= EARLY_PLANES)
    def _():
        stage(page_prompt, pool_keys, pool_values, suffix_keys, suffix_values, out, *scratch)


def copy_kernel(shifted, out):
    rows = shifted[...]
    for chip in range(PLANE):
        out[chip] = rows


def attend_kernel(page_prompt, suffix_len, chip_of, queries, held, got, out, scores,
                  suffix_scores, *buffers):
    top, peak, total, acc = (buffers[i * KVH:(i + 1) * KVH] for i in range(4))
    prefix = lax.axis_index("prefix")
    plane = lax.axis_index("sample")
    core = lax.rem(prefix, CORES)
    sign = 1 - 2 * core
    query_first = jnp.where(core == 0, QUERY_FIRST[0], QUERY_FIRST[1])
    sum_first = jnp.where(core == 0, SUM_FIRST[0], SUM_FIRST[1])
    for a in range(KVH):
        top[a][:PROMPTS] = jnp.full((PROMPTS, HEAD_ROWS, HD), NEG, F32)
        total[a][:PROMPTS] = jnp.zeros((PROMPTS, HEAD_ROWS, HD), F32)
        acc[a][:PROMPTS] = jnp.zeros((PROMPTS, HEAD_ROWS, HD), F32)

    prompts = [page_prompt[slot] for slot in range(OWN)]
    for slot in range(OWN):
        mark = got[slot, pl.ds(MARK_ROW, 16), pl.ds(0, HD)].astype(F32)
        prompts.append(jnp.max(mark).astype(jnp.int32))
    prompts = [jnp.where(prompt >= 0, prompt, PROMPTS) for prompt in prompts]

    own_prompt = lax.div(plane, 4)
    quarter = lax.rem(plane, 4)
    row = lax.broadcasted_iota(jnp.int32, (16, PAGE), 0)
    token = lax.broadcasted_iota(jnp.int32, (16, PAGE), 1)
    token_sample = token >> 5
    length = jnp.where(
        token_sample == 0, suffix_len[0],
        jnp.where(token_sample == 1, suffix_len[1],
                  jnp.where(token_sample == 2, suffix_len[2], suffix_len[3])))
    own_rows = pl.ds(pl.multiple_of(quarter * 16, 16), 16)

    def live(part):
        owner = prefix if part == 0 else prefix + sign
        position = owner * SPAN + (token & (SPAN - 1))
        return ((row & 3) == token_sample) & (position < length)

    def chip_rows(sample_plane, a):
        chip = chip_of[(sign * (plane - sample_plane)) & (DEPTH - 1)]
        return queries[(chip - query_first) & (PLANE - 1), pl.ds(a * 16, 16), :]

    def query_rows(prompt, a):
        return jnp.concatenate([chip_rows(prompt * 4 + q, a) for q in range(4)], axis=0)

    def dot_keys(rows, key):
        return SCALE * lax.dot_general(
            rows, key, (((1,), (0,)), ((), ())), preferred_element_type=F32)

    for part, pages in enumerate((held, got)):
        for slot in range(part * OWN, (part + 1) * OWN):
            for a in range(KVH):
                key = pages[slot % OWN, pl.ds(KEY_ROW, PAGE), pl.ds(a * HD, HD)]
                s = dot_keys(query_rows(prompts[slot], a), key)
                scores[slot, a] = s
                top[a][prompts[slot]] = jnp.maximum(top[a][prompts[slot]], s)

    for part, pages in enumerate((held, got)):
        mask = live(part)
        for a in range(KVH):
            key = pages[:, pl.ds(SUFFIX_KEY_ROW, SPAN), pl.ds(a * HD, HD)]
            key = key.reshape(HD, OWN * SPAN)
            s = jnp.where(mask, dot_keys(chip_rows(plane, a), key), NEG)
            suffix_scores[part, a] = s
            top[a][own_prompt, own_rows] = jnp.maximum(top[a][own_prompt, own_rows], s)

    for a in range(KVH):
        for prompt in range(PROMPTS):
            best = jnp.max(top[a][prompt], axis=1, keepdims=True)
            best = best.astype(BF16).astype(F32)
            peak[a][prompt] = jnp.broadcast_to(best, (HEAD_ROWS, HD))

    for part, pages in enumerate((held, got)):
        for slot in range(part * OWN, (part + 1) * OWN):
            prompt = prompts[slot]
            for a in range(KVH):
                value = pages[slot % OWN, pl.ds(VALUE_ROW, PAGE), pl.ds(a * HD, HD)]
                w = jnp.exp2(scores[slot, a] - peak[a][prompt])
                total[a][prompt] += w
                acc[a][prompt] += jnp.dot(w.astype(BF16), value, preferred_element_type=F32)

    for part, pages in enumerate((held, got)):
        mask = live(part)
        for a in range(KVH):
            value = pages[:, pl.ds(SUFFIX_VALUE_ROW, SPAN), pl.ds(a * HD, HD)]
            value = value.reshape(OWN * SPAN, HD)
            w = jnp.exp2(suffix_scores[part, a] - peak[a][own_prompt, own_rows])
            w = jnp.where(mask, w, 0.0)
            total[a][own_prompt, own_rows] += w
            acc[a][own_prompt, own_rows] += jnp.dot(
                w.astype(BF16), value, preferred_element_type=F32)

    lane = lax.broadcasted_iota(jnp.int32, (HEAD_ROWS, HD), 1)

    for a in range(KVH):
        stats = jnp.zeros((HEAD_ROWS, HD), F32)
        for prompt in range(PROMPTS):
            low = jnp.sum(total[a][prompt], axis=1, keepdims=True)
            high = low.astype(BF16).astype(F32)
            stats = jnp.where(lane == prompt, peak[a][prompt], stats)
            stats = jnp.where(lane == 4 + prompt, high, stats)
            stats = jnp.where(lane == 8 + prompt, low - high, stats)
        for half in range(2):
            def quarter_rows(tile, q):
                return tile[q * 16 + half * 8:q * 16 + half * 8 + 8]
            owner = (a * 2 + half - sum_first) & (PLANE - 1)
            for prompt in range(PROMPTS):
                sums = acc[a][prompt]
                rows = jnp.concatenate([quarter_rows(sums, q) for q in range(4)], axis=0)
                out[owner, pl.ds(prompt * 32, 32), :] = rows.astype(BF16)
            packed = jnp.concatenate(
                [quarter_rows(stats, q) + pltpu.roll(quarter_rows(stats, q + 1), 16, 1)
                 for q in (0, 2)], axis=0)
            out[owner, pl.ds(ROWS, STAT_ROWS), :] = packed.astype(BF16)


def tree_sum(terms):
    while len(terms) > 1:
        terms = [a + b for a, b in zip(terms[::2], terms[1::2])]
    return terms[0]


def plane_kernel(got, out):
    stats = [got[src, pl.ds(ROWS, STAT_ROWS), :].astype(F32) for src in range(PLANE)]
    best = functools.reduce(jnp.maximum, stats)
    weights = [jnp.exp2(jnp.minimum(stat - best, 0.0)) for stat in stats]
    def column(tile, prompt, quarter):
        rows, start = quarter // 2 * 8, quarter % 2 * 16 + prompt
        return tile[rows:rows + 8, start:start + 1]

    denominator = tree_sum([
        weight * (pltpu.roll(stat, HD - 4, 1) + pltpu.roll(stat, HD - 8, 1))
        for weight, stat in zip(weights, stats)])
    sums = []
    for prompt in range(PROMPTS):
        tiles = [got[src, pl.ds(prompt * 32, 32), :].astype(F32) for src in range(PLANE)]
        for quarter in range(4):
            rows = slice(quarter * 8, quarter * 8 + 8)
            sums.append(tree_sum([tile[rows] * column(weight, prompt, quarter)
                                  for tile, weight in zip(tiles, weights)]))
    high = denominator.astype(BF16).astype(F32)
    lane = lax.broadcasted_iota(jnp.int32, (8, HD), 1)
    for prompt in range(PROMPTS):
        for quarter in range(4):
            i = prompt * 4 + quarter
            stat = jnp.where(
                lane == 0, column(best, prompt, quarter),
                jnp.where(lane == 1, column(high, prompt, quarter),
                          column(denominator - high, prompt, quarter)))
            out[PLANE_GROUP.index(i)] = jnp.concatenate([sums[i], stat], axis=0).astype(BF16)


def final_kernel(got, out):
    tiles = [got[src].astype(F32) for src in range(DEPTH)]
    best = tiles[0][8:16]
    for src in range(1, DEPTH):
        best = jnp.maximum(best, tiles[src][8:16])
    best = best[:, 0:1]
    denominator = jnp.zeros((8, 1), F32)
    numerator = jnp.zeros((8, HD), F32)
    for tile in tiles:
        stat = tile[8:16]
        weight = jnp.exp2(stat[:, 0:1] - best)
        denominator = denominator + weight * (stat[:, 1:2] + stat[:, 2:3])
        numerator = numerator + weight * tile[0:8]
    mixed = (numerator / denominator).astype(BF16)
    out[...] = jnp.concatenate([mixed[0:4], mixed[4:8]], axis=1)


SMEM = pl.BlockSpec(memory_space=pltpu.SMEM)
VMEM = pl.BlockSpec(memory_space=pltpu.VMEM)
ANY = pl.BlockSpec(memory_space=pl.ANY)


def budget(mib):
    return pltpu.CompilerParams(vmem_limit_bytes=int(mib * MIB))


def chip_groups(first):
    return [[(first[core] + i) % PLANE * CORES + core for i in range(PLANE)]
            for core in range(CORES)]


def body(queries, pool_keys, pool_values, page_prompt, suffix_keys, suffix_values, suffix_len):
    def pages():
        return tuple(
            pltpu.with_memory_space_constraint(array, pltpu.HBM)
            for array in (page_prompt, pool_keys, pool_values, suffix_keys, suffix_values))

    room = [
        pltpu.VMEM((OWN, PAGE, KVH * HD), BF16),
        pltpu.VMEM((OWN, SPAN, KVH * HD), BF16),
        pltpu.SMEM((OWN,), jnp.int32),
        pltpu.SemaphoreType.DMA((5,)),
    ]
    held_shape = jax.ShapeDtypeStruct((OWN, SEND_ROWS, KVH * HD), BF16)
    own_queries, held = pl.pallas_call(
        query_kernel,
        out_shape=(jax.ShapeDtypeStruct((ROWS, HD), BF16), held_shape),
        in_specs=[ANY] * 6,
        out_specs=(VMEM, VMEM),
        scratch_shapes=[pltpu.VMEM((OWN, H * HD), BF16), pltpu.SemaphoreType.DMA] + room,
        compiler_params=budget(6),
        name="query",
    )(pltpu.with_memory_space_constraint(queries, pltpu.HBM), *pages())
    held = pl.pallas_call(
        stage_kernel,
        out_shape=held_shape,
        in_specs=[ANY] * 5 + [VMEM],
        out_specs=VMEM,
        input_output_aliases={5: 0},
        scratch_shapes=room,
        compiler_params=budget(6),
        name="stage",
    )(*pages(), held)
    shifted = lax.ppermute(
        own_queries, ("prefix", "sample"),
        [((chip * CORES + core) * DEPTH + z, (chip * CORES + core) * DEPTH + (z + (1 - 2 * core) * DISTANCE_OF[chip]) % DEPTH)
         for chip in range(PLANE) for core in range(CORES) for z in range(DEPTH)])
    got = lax.ppermute(held, "prefix", [(i, i ^ 1) for i in range(CORES * PLANE)])
    copies = pl.pallas_call(
        copy_kernel,
        out_shape=jax.ShapeDtypeStruct((PLANE, ROWS, HD), BF16),
        in_specs=[VMEM],
        out_specs=VMEM,
        compiler_params=budget(2),
        cost_estimate=pl.CostEstimate(flops=10**11, transcendentals=0, bytes_accessed=MIB),
        name="copies",
    )(shifted)
    every_query = lax.all_to_all(
        copies, "prefix", 0, 0, axis_index_groups=chip_groups(QUERY_FIRST))
    chip_of = jnp.array([CHIP_OF[distance] for distance in range(DEPTH)], jnp.int32)
    partial = pl.pallas_call(
        attend_kernel,
        out_shape=jax.ShapeDtypeStruct((PLANE, BLOCK_ROWS, HD), BF16),
        in_specs=[SMEM, SMEM, SMEM, VMEM, VMEM, VMEM],
        out_specs=VMEM,
        scratch_shapes=[
            pltpu.VMEM((2 * OWN, KVH, HEAD_ROWS, PAGE), F32),
            pltpu.VMEM((2, KVH, 16, PAGE), F32),
        ] + [pltpu.VMEM((PROMPTS + 1, HEAD_ROWS, HD), F32)] * (4 * KVH),
        compiler_params=budget(18),
        name="attend",
    )(page_prompt, suffix_len, chip_of, every_query, held, got)
    partial = lax.all_to_all(partial, "prefix", 0, 0, axis_index_groups=chip_groups(SUM_FIRST))
    summed = pl.pallas_call(
        plane_kernel,
        out_shape=jax.ShapeDtypeStruct((DEPTH, 16, HD), BF16),
        in_specs=[VMEM],
        out_specs=VMEM,
        compiler_params=budget(4),
        name="plane",
    )(partial)
    summed = lax.all_to_all(summed, "sample", 0, 0, axis_index_groups=[list(PLANE_GROUP)])
    return pl.pallas_call(
        final_kernel,
        out_shape=jax.ShapeDtypeStruct((OWN, 2 * HD), BF16),
        in_specs=[VMEM],
        out_specs=VMEM,
        compiler_params=budget(2),
        name="final",
    )(summed)


def solution(mesh):
    placed = (
        P("sample", None),
        P(("prefix", "sample"), None, None),
        P(("prefix", "sample"), None, None),
        P(("prefix", "sample")),
        P("sample", "prefix", None),
        P("sample", "prefix", None),
        P("sample"),
    )
    return jax.shard_map(
        body, mesh=mesh, in_specs=placed, out_specs=P("sample", "prefix"), check_vma=False
    )
```
